256 devices in a mesh: space: 16 (over z_hi, y), src: 16 (over x, z_lo, core).
Axes of the slice: x: 4, y: 4, z: 8 (z_hi: 4, z_lo: 2; z = z_hi * 2 + z_lo), core: 2. Of those that a mesh axis runs over, the one named last changes fastest.
Arguments:
- fields: float32 [6, 125, 16, 16, 256], P(None, None, 'src', 'space'), may hold values from -6 to 6
- cotangent: float32 [6, 125, 16, 16, 256], P(None, None, 'src', 'space'), may hold values from -1.5 to 1.5
- permittivity: float32 [16, 256], P('space'), may hold values from 1 to 4
- regions: int32 [16, 256], P('space'), may hold values from 0 to 7
- conductance: float32 [8], replicated, may hold values from 2 to 20
- src_layer: int32 [16], P('src'), may hold values from 0 to 15
- src_cell: int32 [16], P('src'), may hold values from 0 to 255
- src_node: int32 [16], P('src'), may hold values from 0 to 124
- src_amp: float32 [16, 6], P('src'), may hold values from -600 to 600
Outputs:
- adjoint: float32 [6, 125, 16, 16, 256], P(None, None, 'src', 'space')
- gradient: float32 [16, 256], P('space')
The draws below stay inside these ranges and needn't reach their ends.
All inputs are finite; a program needn't handle non-finite values.
Results may differ from the reference program's by a relative error of at most 0.0003.
Values sent between devices are 32-bit elements; how exact they have to be, the bound alone decides.
No kernel may reach another device: no remote copies, remote signals or barrier semaphores. Data moves between devices by JAX's collectives and lax.ppermute only.
A program may use at most 128 MiB of HBM per device.

```python
import math
import jax
import jax.numpy as jnp
import numpy as np
from jax import lax

EZ = 16
STEPS = 2
REGIONS = 8
NEX = 16
CELLS_YZ = 256
SOURCES = 16


def set_ends(drawn, rng, low, largest):
    spot = [jax.random.randint(jax.random.fold_in(rng, axis), (), 0, length) for axis, length in enumerate(drawn.shape)]
    main_axis = drawn.shape.index(max(drawn.shape))
    beside = spot[:main_axis] + [(spot[main_axis] + 1) % drawn.shape[main_axis]] + spot[main_axis + 1:]
    return drawn.at[tuple(spot)].set(low).at[tuple(beside)].set(largest)


def level_of(stream_key, shape, split, low, largest):
    gain, own = 1.0, jax.random.fold_in(stream_key, 6)
    for position, parts in split:
        heights = jnp.exp(jax.random.uniform(jax.random.fold_in(own, position), (parts,), jnp.float32, low / len(split), largest / len(split)))
        gain = gain * jnp.repeat(heights, shape[position] // parts).reshape([-1 if axis == position else 1 for axis in range(len(shape))])
    return gain


def gaussian(own_key, shape, width, bound, split=(), held_as=jnp.bfloat16):
    values = width * jax.random.normal(own_key, shape, jnp.float32)
    if split:
        values = values * level_of(own_key, shape, split, -0.22, 0.18)
    return jnp.clip(values, -bound, bound).astype(held_as)


def setup_inputs(seed: int = 0) -> dict:
    streams_of = jax.random.split(jax.random.key(seed), 10)
    fields = gaussian(streams_of[0], (6, 125, SOURCES, NEX, CELLS_YZ), 1.0, 6.0, ((2, 16), (3, 16)), jnp.float32)
    cotangent = gaussian(streams_of[1], (6, 125, SOURCES, NEX, CELLS_YZ), 0.25, 1.5, ((2, 16), (3, 16)), jnp.float32)
    permittivity = jnp.clip(jnp.exp(math.log(4.0) - 1.3862944 * jax.random.uniform(streams_of[2], (NEX, CELLS_YZ), jnp.float32) ** level_of(streams_of[2], (NEX, CELLS_YZ), ((0, 16),), -0.2, 0.2)), 1.0, 4.0)
    regions = set_ends(jax.random.randint(streams_of[3], (NEX, CELLS_YZ), 0, REGIONS), jax.random.fold_in(streams_of[3], 1), 0, REGIONS - 1).astype(jnp.int32)
    conductance = jnp.clip(jnp.exp(jax.random.uniform(streams_of[4], (REGIONS,), jnp.float32, math.log(2.0), math.log(20.0))), 2.0, 20.0)
    src_layer = set_ends(jax.random.randint(streams_of[5], (SOURCES,), 0, NEX), jax.random.fold_in(streams_of[5], 1), 0, NEX - 1).astype(jnp.int32)
    src_cell = set_ends(jax.random.randint(streams_of[6], (SOURCES,), 0, CELLS_YZ), jax.random.fold_in(streams_of[6], 1), 0, CELLS_YZ - 1).astype(jnp.int32)
    src_node = set_ends(jax.random.randint(streams_of[7], (SOURCES,), 0, 125), jax.random.fold_in(streams_of[7], 1), 0, 124).astype(jnp.int32)
    src_amp = gaussian(streams_of[8], (SOURCES, 3 * STEPS), 100.0, 600.0, ((0, 16),), jnp.float32)
    return dict(fields=fields, cotangent=cotangent, permittivity=permittivity, regions=regions, conductance=conductance, src_layer=src_layer, src_cell=src_cell, src_node=src_node, src_amp=src_amp)


TIME_STEP = 0.02
PENALTY = 1.0
LIFT_SCALE = 20.0
METRIC = 2.0

def gll_derivative():
    points = np.array([-1.0, -math.sqrt(3.0 / 7.0), 0.0, math.sqrt(3.0 / 7.0), 1.0])
    products = np.array([np.prod([points[row_index] - points[column_index] for column_index in range(5) if column_index != row_index]) for row_index in range(5)])
    matrix = np.zeros((5, 5))
    for row_index in range(5):
        for column_index in range(5):
            if column_index != row_index:
                matrix[row_index, column_index] = products[row_index] / (products[column_index] * (points[row_index] - points[column_index]))
    for row_index in range(5):
        matrix[row_index, row_index] = -np.sum(matrix[row_index])
    return matrix

def derive(values, direction):
    matrix = jnp.asarray(gll_derivative() * METRIC, dtype=jnp.float32)
    patterns = ('ij,cj...->ci...', 'ij,caj...->cai...', 'ij,cabj...->cabi...')
    return jnp.einsum(patterns[direction], matrix, values, precision=lax.Precision.HIGHEST)

def curl(values):
    first_slope = derive(values, 0)
    second_slope = derive(values, 1)
    third_slope = derive(values, 2)
    return jnp.stack([second_slope[2] - third_slope[1], third_slope[0] - first_slope[2], first_slope[1] - second_slope[0]])

def face_slice(values, normal_axis, face_side):
    face_node = 0 if face_side == 0 else 4
    if normal_axis == 0:
        return values[:, face_node]
    if normal_axis == 1:
        return values[:, :, face_node]
    return values[:, :, :, face_node]

def face_add(values, normal_axis, face_side, addend):
    face_node = 0 if face_side == 0 else 4
    if normal_axis == 0:
        return values.at[:, face_node].add(addend)
    if normal_axis == 1:
        return values.at[:, :, face_node].add(addend)
    return values.at[:, :, :, face_node].add(addend)

def outside(values, outer, normal_axis, face_side):
    if normal_axis == 0:
        if face_side == 0:
            return jnp.concatenate([outer[..., :1, :], face_slice(values, 0, 1)[..., :-1, :]], axis=-2)
        return jnp.concatenate([face_slice(values, 0, 0)[..., 1:, :], outer[..., 1:, :]], axis=-2)
    facing = face_slice(values, normal_axis, 1 - face_side)
    if normal_axis == 1:
        return jnp.roll(facing, EZ if face_side == 0 else -EZ, axis=-1)
    column = jnp.arange(facing.shape[-1], dtype=jnp.int32) % EZ
    if face_side == 0:
        return jnp.where(column == 0, jnp.roll(facing, 1 - EZ, axis=-1), jnp.roll(facing, 1, axis=-1))
    return jnp.where(column == EZ - 1, jnp.roll(facing, EZ - 1, axis=-1), jnp.roll(facing, -1, axis=-1))

def normal_cross(normal_axis, normal_sign, vector):
    empty = jnp.zeros_like(vector[0])
    if normal_axis == 0:
        pieces = [empty, -vector[2], vector[1]]
    elif normal_axis == 1:
        pieces = [vector[2], empty, -vector[0]]
    else:
        pieces = [-vector[1], vector[0], empty]
    return normal_sign * jnp.stack(pieces)

def double_cross(normal_axis, vector):
    pieces = [jnp.zeros_like(vector[0]) if component == normal_axis else -vector[component] for component in range(3)]
    return jnp.stack(pieces)

def rhs_field(curled, penalised, outer_curled, outer_penalised, orient):
    result = orient * curl(curled)
    for normal_axis in range(3):
        for face_side in range(2):
            normal_sign = -1.0 if face_side == 0 else 1.0
            jump_curled = face_slice(curled, normal_axis, face_side) - outside(curled, outer_curled, normal_axis, face_side)
            jump_penalised = face_slice(penalised, normal_axis, face_side) - outside(penalised, outer_penalised, normal_axis, face_side)
            face_flux = -0.5 * orient * normal_cross(normal_axis, normal_sign, jump_curled) + 0.5 * PENALTY * double_cross(normal_axis, jump_penalised)
            result = face_add(result, normal_axis, face_side, LIFT_SCALE * face_flux)
    return result

def conductivity(regions, conductance):
    matches = regions[..., None] == jnp.arange(conductance.shape[0], dtype=jnp.int32)
    return lax.optimization_barrier(jnp.sum(jnp.where(matches, conductance, 0.0), axis=-1))

def source_terms(layer_index, cell_index, node_index, amplitude, layers, cell_count):
    layer_match = (layer_index[:, None] == jnp.arange(layers, dtype=jnp.int32)[None, :]).astype(jnp.float32)
    cell_match = (cell_index[:, None] == jnp.arange(cell_count, dtype=jnp.int32)[None, :]).astype(jnp.float32)
    node_match = (node_index[:, None] == jnp.arange(125, dtype=jnp.int32)[None, :]).astype(jnp.float32)
    placed = node_match.T[:, :, None, None] * (layer_match[:, :, None] * cell_match[:, None, :])[None]
    source_list = []
    for time_index in range(amplitude.shape[1] // 3):
        weights = amplitude[:, 3 * time_index:3 * time_index + 3].T
        source_term = weights[:, None, :, None, None] * placed[None]
        source_list.append(source_term.reshape((3, 5, 5, 5) + placed.shape[1:]))
    return source_list

def forward(fields_now, permittivity, damping, source_list):
    electric, magnetic = (fields_now[:3], fields_now[3:])
    exterior = jnp.zeros((3, 5, 5, fields_now.shape[4], 2, fields_now.shape[6]), jnp.float32)
    for time_index in range(len(source_list)):
        magnetic_next = magnetic + TIME_STEP * rhs_field(electric, magnetic, exterior, exterior, -1.0)
        forcing = rhs_field(magnetic_next, electric, exterior, exterior, 1.0) - damping * electric + source_list[time_index]
        electric = electric + TIME_STEP / permittivity * forcing
        magnetic = magnetic_next
    return jnp.concatenate([electric, magnetic], axis=0)

def reference(fields, cotangent, permittivity, regions, conductance, src_layer, src_cell, src_node, src_amp):
    damping = conductivity(regions, conductance)
    moved_fields = jnp.moveaxis(fields, 2, 0)
    moved_cotangent = jnp.moveaxis(cotangent, 2, 0)

    def per_source(running, inputs):
        one_field, one_cotangent, layer_one, cell_one, node_one, amp_one = inputs
        nodal_shape = (6, 5, 5, 5, 1) + one_field.shape[2:]
        initial = one_field.reshape(nodal_shape)
        source_list = source_terms(layer_one[None], cell_one[None], node_one[None], amp_one[None], NEX, CELLS_YZ)

        def evolve(fields_now, permittivity_now):
            return forward(fields_now, permittivity_now, damping, source_list)
        unused, pullback = jax.vjp(evolve, initial, permittivity)
        back_fields, back_permittivity = pullback(one_cotangent.reshape(nodal_shape))
        return (running + back_permittivity, back_fields.reshape(one_field.shape))
    gradient, adjoint = lax.scan(per_source, jnp.zeros_like(permittivity), (moved_fields, moved_cotangent, src_layer, src_cell, src_node, src_amp))
    return (jnp.moveaxis(adjoint, 0, 2), gradient)
```

```python
import functools
import math

import jax
import jax.numpy as jnp
import numpy as np
from jax import lax
from jax.experimental import pallas as pl
from jax.experimental.pallas import tpu as pltpu
from jax.sharding import PartitionSpec as P

EZ = 16
DT = 0.02
LIFT = 10.0
METRIC = 2.0
F32 = jnp.float32


WEIGHTS = (1.0 / 10.0, 49.0 / 90.0, 32.0 / 45.0, 49.0 / 90.0, 1.0 / 10.0)


def central_matrix():
    points = np.array([-1.0, -math.sqrt(3.0 / 7.0), 0.0, math.sqrt(3.0 / 7.0), 1.0])
    products = [
        np.prod([points[i] - points[j] for j in range(5) if j != i]) for i in range(5)
    ]
    matrix = np.zeros((5, 5))
    for i in range(5):
        for j in range(5):
            if j != i:
                matrix[i, j] = products[i] / (products[j] * (points[i] - points[j]))
    for i in range(5):
        matrix[i, i] = -np.sum(matrix[i])
    return METRIC * matrix + np.diag([LIFT, 0.0, 0.0, 0.0, -LIFT])


CENTRAL = central_matrix()


def derive(u):
    d = CENTRAL
    e0, e1, m = u[0] + u[4], u[1] + u[3], u[2]
    o0, o1 = u[0] - u[4], u[1] - u[3]
    h = lambda i, j: float(0.5 * (d[i, j] - d[i, 4 - j]))
    g = lambda i, j: float(0.5 * (d[i, j] + d[i, 4 - j]))
    s0 = h(0, 0) * o0 + h(0, 1) * o1
    s1 = h(1, 0) * o0 + h(1, 1) * o1
    d0 = g(0, 0) * e0 + g(0, 1) * e1 + float(d[0, 2]) * m
    d1 = g(1, 0) * e0 + g(1, 1) * e1 + float(d[1, 2]) * m
    mid = float(d[2, 0]) * o0 + float(d[2, 1]) * o1
    return [s0 + d0, s1 + d1, mid, s1 - d1, s0 - d0]


def swap4(x):
    return pltpu.roll(x, 4, 0)


def iotas():
    row = lax.broadcasted_iota(jnp.int32, (8, 128), 0)
    lane = lax.broadcasted_iota(jnp.int32, (8, 128), 1)
    return row, lane


def rows(row, v0, v1, v2, v3):
    return jnp.where(row < 2, v0, jnp.where(row < 4, v1, jnp.where(row < 6, v2, v3)))


class Cells:
    def __init__(self, row, lane):
        self.even = (row & 1) == 0
        self.y_last = lane >= 112
        self.y_first = lane < 16
        self.z_last = (lane & 15) == 15
        self.z_first = (lane & 15) == 0

    def other_half(self, x):
        return jnp.where(self.even, pltpu.roll(x, 7, 0), pltpu.roll(x, 1, 0))

    def y_up(self, x):
        x = pltpu.roll(x, 112, 1)
        return jnp.where(self.y_last, self.other_half(x), x)

    def y_down(self, x):
        x = pltpu.roll(x, 16, 1)
        return jnp.where(self.y_first, self.other_half(x), x)

    def z_up(self, x):
        return jnp.where(self.z_last, pltpu.roll(x, 15, 1), pltpu.roll(x, 127, 1))

    def z_down(self, x):
        return jnp.where(self.z_first, pltpu.roll(x, 113, 1), pltpu.roll(x, 1, 1))


def weight(i, inverse=False):
    w = [1.0 / v if inverse else v for v in WEIGHTS]
    return jnp.where((i == 0) | (i == 4), w[0], jnp.where(i == 2, w[2], w[1])).astype(F32)


def penalty(inner, outer):
    return swap4(LIFT * (outer - inner))


def x_pass(s, t_ref, m_t, ext):
    def body(b, carry):
        for c in range(5):
            n = [25 * a + 5 * b + c for a in range(5)]
            y = [s[1, n[a]] * m_t for a in range(5)]
            z = [s[2, n[a]] * m_t for a in range(5)]
            dy, dz = derive(y), derive(z)
            for a in range(5):
                out_y, out_z = -dz[a], dy[a]
                if a in (0, 4):
                    out_y = out_y - swap4(LIFT * y[a])
                    out_z = out_z - swap4(LIFT * z[a])
                    if ext is not None:
                        more_y, more_z = ext(a, 5 * b + c)
                        out_y, out_z = out_y + more_y, out_z + more_z
                t_ref[1, n[a]] = out_y
                t_ref[2, n[a]] = out_z
        return carry

    lax.fori_loop(0, 5, body, 0)


def y_pass(s, t_ref, m_t, cells):
    def body(a, carry):
        for c in range(5):
            n = [25 * a + 5 * b + c for b in range(5)]
            z = [s[2, n[b]] * m_t for b in range(5)]
            x = [s[0, n[b]] * m_t for b in range(5)]
            dz, dx = derive(z), derive(x)
            for b in range(5):
                out_x = dz[b]
                out_z = t_ref[2, n[b]] - dx[b]
                if b == 0:
                    oz, ox = cells.y_down(z[4]), cells.y_down(x[4])
                    out_x = out_x - LIFT * oz + penalty(x[0], ox)
                    out_z = out_z + LIFT * ox + penalty(z[0], oz)
                if b == 4:
                    oz, ox = cells.y_up(z[0]), cells.y_up(x[0])
                    out_x = out_x + LIFT * oz + penalty(x[4], ox)
                    out_z = out_z - LIFT * ox + penalty(z[4], oz)
                t_ref[0, n[b]] = out_x
                t_ref[2, n[b]] = out_z
        return carry

    lax.fori_loop(0, 5, body, 0)


def z_pass(s, t_ref, m_t, m_s, m_f, cells, out, carry):
    def body(a, carry):
        for b in range(5):
            n = [25 * a + 5 * b + c for c in range(5)]
            s_x = [s[0, n[c]] for c in range(5)]
            s_y = [s[1, n[c]] for c in range(5)]
            x = [v * m_t for v in s_x]
            y = [v * m_t for v in s_y]
            dx, dy = derive(x), derive(y)
            for c in range(5):
                out_y = t_ref[1, n[c]] + dx[c]
                out_x = t_ref[0, n[c]] - dy[c]
                if c == 0:
                    ox, oy = cells.z_down(x[4]), cells.z_down(y[4])
                    out_y = out_y - LIFT * ox + penalty(y[0], oy)
                    out_x = out_x + LIFT * oy + penalty(x[0], ox)
                if c == 4:
                    ox, oy = cells.z_up(x[0]), cells.z_up(y[0])
                    out_y = out_y + LIFT * ox + penalty(y[4], oy)
                    out_x = out_x - LIFT * oy + penalty(x[4], ox)
                for comp, old, got in (
                    (0, s_x[c], out_x),
                    (1, s_y[c], out_y),
                    (2, s[2, n[c]], t_ref[2, n[c]]),
                ):
                    inc = swap4(got) * m_f + old * m_s
                    carry = out(comp, a, b, c, n[c], old, inc, carry)
        return carry

    return lax.fori_loop(0, 5, body, carry)


def materials(perm_ref, reg_ref, cond_ref):
    two = lambda x: jnp.concatenate([x, x, x, x], axis=0)
    perm = perm_ref[...]
    reg = reg_ref[...]
    damping = jnp.zeros((2, 128), F32)
    for r in range(8):
        damping = jnp.where(reg == r, cond_ref[r], damping)
    coef = DT / perm
    return two(coef), two(damping)


def masks(parity, row, coef, damping):
    if parity == 1:
        m_t = rows(row, 1.0, coef, -1.0, 0.0)
        m_f = rows(row, 0.0, 1.0, -DT, 1.0)
        m_s = rows(row, 0.0, -damping * coef, 0.0, 0.0)
    else:
        m_t = rows(row, 1.0, 0.0, 1.0, DT)
        m_f = rows(row, coef, -1.0, 0.0, 1.0)
        m_s = rows(row, -damping * coef, 0.0, 0.0, 0.0)
    return m_t, m_f, m_s


def first_traces(s, lo_ref, hi_ref, m_t, row):
    def body(b, carry):
        for c in range(5):
            k = 5 * b + c
            for a, sign, ref in ((0, 1.0, lo_ref), (4, -1.0, hi_ref)):
                y, z = s[1, 25 * a + k] * m_t, s[2, 25 * a + k] * m_t
                ref[0, k] = jnp.where(row < 2, sign * z - swap4(y), y)
                ref[1, k] = jnp.where(row < 2, -sign * y - swap4(z), z)
        return carry

    lax.fori_loop(0, 5, body, 0)


def second_traces(s, lo_ref, hi_ref, row):
    def body(b, carry):
        for c in range(5):
            k = 5 * b + c
            for a, sign, ref in ((0, 1.0, lo_ref), (4, -1.0, hi_ref)):
                y, z = s[1, 25 * a + k], s[2, 25 * a + k]
                out_y = jnp.where(row < 6, swap4(y) - sign * z, DT * y)
                out_z = jnp.where(row < 6, swap4(z) + sign * y, DT * z)
                ref[0, k] = jnp.where(row < 4, ref[0, k], out_y)
                ref[1, k] = jnp.where(row < 4, ref[1, k], out_z)
        return carry

    lax.fori_loop(0, 5, body, 0)


def odd_level(s, t_ref, lo_ref, hi_ref, row, coef, damping, cells):
    m_t, m_f, m_s = masks(1, row, coef, damping)
    first_traces(s, lo_ref, hi_ref, m_t, row)
    x_pass(s, t_ref, m_t, None)
    y_pass(s, t_ref, m_t, cells)

    def out(comp, a, b, c, n, old, inc, carry):
        s[comp, n] = old + inc
        return carry

    z_pass(s, t_ref, m_t, m_s, m_f, cells, out, 0)
    second_traces(s, lo_ref, hi_ref, row)


def outer_parts(s_in, s, below, above, lo_own, hi_own, row, coef, damping):
    position, last = lax.axis_index("space"), lax.axis_size("space") - 1
    has = {0: (position > 0).astype(F32), 4: (position < last).astype(F32)}
    to_same = rows(row, 0.0, LIFT, 0.0, 0.0)
    to_primal = rows(row, 0.0, 0.0, LIFT * DT, 0.0)
    to_dual = rows(row, 0.0, 0.0, 0.0, LIFT)
    level_two = row >= 4
    late_primal = rows(row, 0.0, 0.0, LIFT, 0.0)
    late_dual = rows(row, 0.0, 0.0, 0.0, LIFT)
    fix = rows(row, -LIFT * DT, LIFT * DT, 0.0, 0.0)
    sides = ((0, -1.0, below, lo_own), (4, 1.0, above, hi_own))

    def body(b, carry):
        for c in range(5):
            k = 5 * b + c
            for a, sign, got, own in sides:
                y, z = got[0, k] * has[a], got[1, k] * has[a]
                ry, rz = swap4(y), swap4(z)
                n = 25 * a + k
                s[1, n] = s_in[1, n] + (ry * to_primal - sign * (rz * to_dual) + y * to_same)
                s[2, n] = s_in[2, n] + (rz * to_primal + sign * (ry * to_dual) + z * to_same)
        return carry

    lax.fori_loop(0, 5, body, 0)

    def ext(a, k):
        _, sign, got, own = sides[0 if a == 0 else 1]
        y = (got[0, k] + sign * swap4(own[1, k] * fix)) * has[a]
        z = (got[1, k] - sign * swap4(own[0, k] * fix)) * has[a]
        ext_y = y * late_primal - sign * (z * late_dual) + swap4(y * late_dual)
        ext_z = z * late_primal + sign * (y * late_dual) + swap4(z * late_dual)
        return ext_y, ext_z

    return ext


def add_source(s, step, layer_ref, cell_ref, node_ref, amp_ref, row, lane, coef):
    here = layer_ref[0] == lax.axis_index("space")
    cell = cell_ref[0]
    node = node_ref[0]
    place = (row < 2) & ((row & 1) * 128 + lane == cell)
    shape = jnp.where(place, coef, 0.0)
    incs = []
    for comp in range(3):
        inc = shape * jnp.where(here, amp_ref[0, 3 * step + comp], 0.0)
        s[comp, node] = s[comp, node] + inc
        incs.append(inc)
    return node, incs


def first_kernel(
    fields, cot, perm_ref, reg_ref, cond_ref, s, lo_ref, hi_ref, t_ref, sems
):
    row, lane = iotas()
    cells = Cells(row, lane)
    copies = [
        pltpu.make_async_copy(src, s.at[:, :, pl.ds(2 * i, 2), :], sems.at[i])
        for i, src in enumerate(
            (fields.at[0:3], cot.at[0:3], fields.at[3:6], cot.at[3:6])
        )
    ]
    for copy in copies:
        copy.start()
    coef, damping = materials(perm_ref, reg_ref, cond_ref)
    for copy in copies:
        copy.wait()
    dual = (row & 2) != 0

    def scale(a, carry):
        for b in range(5):
            for c in range(5):
                n = 25 * a + 5 * b + c
                w = weight(a, True) * (1.0 / (WEIGHTS[b] * WEIGHTS[c]))
                m = jnp.where(dual, w, 1.0)
                for comp in range(3):
                    s[comp, n] = s[comp, n] * m
        return carry

    lax.fori_loop(0, 5, scale, 0)
    odd_level(s, t_ref, lo_ref, hi_ref, row, coef, damping, cells)


def copy_state(s_in, s):
    def body(a, carry):
        for k in range(25):
            for comp in range(3):
                s[comp, 25 * a + k] = s_in[comp, 25 * a + k]
        return carry

    lax.fori_loop(0, 5, body, 0)


def second_kernel(
    s_in, lo_own, hi_own, below, above, perm_ref, reg_ref, cond_ref, layer_ref,
    cell_ref, node_ref, amp_ref, s, lo_ref, hi_ref, g_ref, t_ref,
):
    row, lane = iotas()
    cells = Cells(row, lane)
    coef, damping = materials(perm_ref, reg_ref, cond_ref)
    copy_state(s_in, s)
    ext = outer_parts(s_in, s, below, above, lo_own, hi_own, row, coef, damping)
    m_t, m_f, m_s = masks(2, row, coef, damping)
    x_pass(s, t_ref, m_t, ext)
    y_pass(s, t_ref, m_t, cells)

    def out(comp, a, b, c, n, old, inc, carry):
        new = old + inc
        s[comp, n] = new
        w = weight(a) * (WEIGHTS[b] * WEIGHTS[c])
        return carry + pltpu.roll(inc, 2, 0) * (new * w)

    total = z_pass(s, t_ref, m_t, m_s, m_f, cells, out, jnp.zeros((8, 128), F32))
    node, incs = add_source(
        s, 0, layer_ref, cell_ref, node_ref, amp_ref, row, lane, coef
    )
    w = weight(node // 25) * weight((node // 5) % 5) * weight(node % 5)
    for comp in range(3):
        total = total + pltpu.roll(incs[comp], 2, 0) * (s[comp, node] * w)
    g_ref[...] = total
    odd_level(s, t_ref, lo_ref, hi_ref, row, coef, damping, cells)


def third_kernel(
    s_in, lo_own, hi_own, below, above, perm_ref, reg_ref, cond_ref, layer_ref,
    cell_ref, node_ref, amp_ref, g_in, cot, adj, g_ref, s, t_ref, c_ref, sems,
):
    row, lane = iotas()
    cells = Cells(row, lane)
    load = pltpu.make_async_copy(cot.at[0:3], c_ref.at[:, :, pl.ds(0, 2), :], sems.at[0])
    load.start()
    coef, damping = materials(perm_ref, reg_ref, cond_ref)
    copy_state(s_in, s)
    ext = outer_parts(s_in, s, below, above, lo_own, hi_own, row, coef, damping)
    m_t, m_f, m_s = masks(2, row, coef, damping)
    x_pass(s, t_ref, m_t, ext)
    y_pass(s, t_ref, m_t, cells)
    load.wait()
    dual = (row & 2) != 0

    def out(comp, a, b, c, n, old, inc, carry):
        w = weight(a) * (WEIGHTS[b] * WEIGHTS[c])
        s[comp, n] = (old + inc) * w
        return carry + inc[0:2] * c_ref[comp, n, 0:2]

    total = z_pass(s, t_ref, m_t, m_s, m_f, cells, out, jnp.zeros((2, 128), F32))
    stores = [
        pltpu.make_async_copy(
            s.at[:, :, pl.ds(2 + 4 * i, 2), :], adj.at[3 * i : 3 * i + 3], sems.at[1 + i]
        )
        for i in range(2)
    ]
    for store in stores:
        store.start()
    here = layer_ref[0] == lax.axis_index("space")
    node = node_ref[0]
    place = (row & 1) * 128 + lane == cell_ref[0]
    shape = jnp.where(place, coef, 0.0)[0:2]
    for comp in range(3):
        amp = jnp.where(here, amp_ref[0, 3 + comp], 0.0)
        total = total + (shape * amp) * c_ref[comp, node, 0:2]
    total = total + g_in[2:4]
    g_ref[...] = -total / perm_ref[...]
    for store in stores:
        store.wait()


def struct(*shape):
    return jax.ShapeDtypeStruct(shape, F32)


VMEM = pl.BlockSpec(memory_space=pltpu.VMEM)
SMEM = pl.BlockSpec(memory_space=pltpu.SMEM)
ANY = pl.BlockSpec(memory_space=pl.ANY)
PARAMS = pltpu.CompilerParams(vmem_limit_bytes=24 * 1024 * 1024)
STATE = (3, 125, 8, 128)
TRACE = (2, 25, 8, 128)


def exchange(lo, hi):
    peers = lax.axis_size("space")
    up = [(i, (i + 1) % peers) for i in range(peers)]
    down = [((i + 1) % peers, i) for i in range(peers)]
    below = lax.ppermute(hi, "space", up)
    above = lax.ppermute(lo, "space", down)
    return below, above


def src_sum(x):
    for group in ((1, 2, 3), (4, 8, 12)):
        got = [lax.ppermute(x, "src", [(i, i ^ d) for i in range(16)]) for d in group]
        x = (x + got[0]) + (got[1] + got[2])
    return x


def on_device(
    fields, cotangent, permittivity, regions, conductance, src_layer, src_cell, src_node, src_amp
):
    wide = fields.shape[:2] + (2, 128)
    f = fields.reshape(wide)
    cot = cotangent.reshape(wide)
    perm = permittivity.reshape(2, 128)
    reg = regions.reshape(2, 128)
    material = (perm, reg, conductance)
    source = (src_layer, src_cell, src_node, src_amp)
    s, lo, hi = pl.pallas_call(
        first_kernel,
        out_shape=(struct(*STATE), struct(*TRACE), struct(*TRACE)),
        in_specs=[ANY, ANY, VMEM, VMEM, SMEM],
        out_specs=[VMEM] * 3,
        scratch_shapes=[pltpu.VMEM(STATE, F32), pltpu.SemaphoreType.DMA((4,))],
        compiler_params=PARAMS,
        name="first",
    )(f, cot, *material)
    below, above = exchange(lo, hi)
    s, lo, hi, g = pl.pallas_call(
        second_kernel,
        out_shape=(struct(*STATE), struct(*TRACE), struct(*TRACE), struct(8, 128)),
        in_specs=[VMEM] * 7 + [SMEM] * 5,
        out_specs=[VMEM] * 4,
        scratch_shapes=[pltpu.VMEM(STATE, F32)],
        compiler_params=PARAMS,
        name="second",
    )(s, lo, hi, below, above, *material, *source)
    below, above = exchange(lo, hi)
    adjoint, g = pl.pallas_call(
        third_kernel,
        out_shape=(struct(*wide), struct(2, 128)),
        in_specs=[VMEM] * 7 + [SMEM] * 5 + [VMEM, ANY],
        out_specs=[ANY, VMEM],
        scratch_shapes=[
            pltpu.VMEM(STATE, F32),
            pltpu.VMEM(STATE, F32),
            pltpu.VMEM(STATE, F32),
            pltpu.SemaphoreType.DMA((3,)),
        ],
        compiler_params=PARAMS,
        name="third",
    )(s, lo, hi, below, above, *material, *source, g, cot)
    gradient = src_sum(g).reshape(permittivity.shape)
    return adjoint.reshape(fields.shape), gradient


def solution(mesh):
    return jax.shard_map(
        on_device,
        mesh=mesh,
        in_specs=(
            P(None, None, "src", "space", None),
            P(None, None, "src", "space", None),
            P("space", None),
            P("space", None),
            P(),
            P("src"),
            P("src"),
            P("src"),
            P("src", None),
        ),
        out_specs=(P(None, None, "src", "space", None), P("space", None)),
        check_vma=False,
    )
```

```python
import math

import jax
import jax.numpy as jnp
import numpy as np
from jax import lax
from jax.experimental import pallas as pl
from jax.experimental.layout import Layout, with_layout_constraint
from jax.experimental.pallas import tpu as pltpu
from jax.sharding import PartitionSpec as P

EZ = 16
DT = 0.02
LIFT = 10.0
METRIC = 2.0
F32 = jnp.float32


WEIGHTS = (1.0 / 10.0, 49.0 / 90.0, 32.0 / 45.0, 49.0 / 90.0, 1.0 / 10.0)


def central_matrix():
    points = np.array([-1.0, -math.sqrt(3.0 / 7.0), 0.0, math.sqrt(3.0 / 7.0), 1.0])
    products = [
        np.prod([points[i] - points[j] for j in range(5) if j != i]) for i in range(5)
    ]
    matrix = np.zeros((5, 5))
    for i in range(5):
        for j in range(5):
            if j != i:
                matrix[i, j] = products[i] / (products[j] * (points[i] - points[j]))
    for i in range(5):
        matrix[i, i] = -np.sum(matrix[i])
    return (METRIC * matrix + np.diag([LIFT, 0.0, 0.0, 0.0, -LIFT])) / LIFT


CENTRAL = central_matrix()


def halves():
    d = CENTRAL
    h = [[float(0.5 * (d[i, j] - d[i, 4 - j])) for j in range(2)] for i in range(2)]
    g = [[float(0.5 * (d[i, j] + d[i, 4 - j])) for j in range(2)] for i in range(2)]
    return h, g, [float(d[i, 2]) for i in range(2)], [float(d[2, j]) for j in range(2)]


ODD, EVEN, MIDDLE, CENTRE = halves()


def derive(u):
    e0, e1, m = u[0] + u[4], u[1] + u[3], u[2]
    o0, o1 = u[0] - u[4], u[1] - u[3]
    s0 = ODD[0][0] * o0 + ODD[0][1] * o1
    s1 = ODD[1][0] * o0 + ODD[1][1] * o1
    d0 = EVEN[0][0] * e0 + EVEN[0][1] * e1 + MIDDLE[0] * m
    d1 = EVEN[1][0] * e0 + EVEN[1][1] * e1 + MIDDLE[1] * m
    mid = CENTRE[0] * o0 + CENTRE[1] * o1
    return [s0 + d0, s1 + d1, mid, s1 - d1, s0 - d0]


def derive_at_ends(u):
    e0, e1, m = u[0] + u[4], u[1] + u[3], u[2]
    o0, o1 = u[0] - u[4], u[1] - u[3]
    s0 = ODD[0][0] * o0 + ODD[0][1] * o1
    d0 = EVEN[0][0] * e0 + EVEN[0][1] * e1 + MIDDLE[0] * m
    return {0: s0 + d0, 4: s0 - d0}


def derive_inside(u):
    e0, e1, m = u[0] + u[4], u[1] + u[3], u[2]
    o0, o1 = u[0] - u[4], u[1] - u[3]
    s1 = ODD[1][0] * o0 + ODD[1][1] * o1
    d1 = EVEN[1][0] * e0 + EVEN[1][1] * e1 + MIDDLE[1] * m
    mid = CENTRE[0] * o0 + CENTRE[1] * o1
    return {1: s1 + d1, 2: mid, 3: s1 - d1}


def derive_from_inside(u):
    e1, o1, m = u[1] + u[3], u[1] - u[3], u[2]
    s0, s1 = ODD[0][1] * o1, ODD[1][1] * o1
    d0 = EVEN[0][1] * e1 + MIDDLE[0] * m
    d1 = EVEN[1][1] * e1 + MIDDLE[1] * m
    return [s0 + d0, s1 + d1, CENTRE[1] * o1, s1 - d1, s0 - d0]


def derive_from_ends(u0, u4):
    e0, o0 = u0 + u4, u0 - u4
    s0, s1 = ODD[0][0] * o0, ODD[1][0] * o0
    d0, d1 = EVEN[0][0] * e0, EVEN[1][0] * e0
    return [s0 + d0, s1 + d1, CENTRE[0] * o0, s1 - d1, s0 - d0]


def swap4(x):
    return pltpu.roll(x, 4, 0)


def iotas():
    row = lax.broadcasted_iota(jnp.int32, (8, 128), 0)
    lane = lax.broadcasted_iota(jnp.int32, (8, 128), 1)
    return row, lane


def rows(row, v0, v1, v2, v3):
    return jnp.where(row < 2, v0, jnp.where(row < 4, v1, jnp.where(row < 6, v2, v3)))


class Cells:
    def __init__(self, row, lane):
        self.even = (row & 1) == 0
        self.y_last = lane >= 112
        self.y_first = lane < 16
        self.z_last = (lane & 15) == 15
        self.z_first = (lane & 15) == 0

    def other_half(self, x):
        return jnp.where(self.even, pltpu.roll(x, 7, 0), pltpu.roll(x, 1, 0))

    def y_up(self, x):
        x = pltpu.roll(x, 112, 1)
        return jnp.where(self.y_last, self.other_half(x), x)

    def y_down(self, x):
        x = pltpu.roll(x, 16, 1)
        return jnp.where(self.y_first, self.other_half(x), x)

    def z_up(self, x):
        return jnp.where(self.z_last, pltpu.roll(x, 15, 1), pltpu.roll(x, 127, 1))

    def z_down(self, x):
        return jnp.where(self.z_first, pltpu.roll(x, 113, 1), pltpu.roll(x, 1, 1))


ENDS, INSIDE = (0, 4), (1, 2, 3)


def node_weight(a, k):
    return WEIGHTS[a] * WEIGHTS[k // 5] * WEIGHTS[k % 5]


def weight_at(i):
    return jnp.where((i == 0) | (i == 4), WEIGHTS[0], jnp.where(i == 2, WEIGHTS[2], WEIGHTS[1]))


def penalty(inner, outer):
    return swap4(outer - inner)


def y_lines(planes, get, add, cells):
    for a in planes:
        for c in range(5):
            z = [get(2, a, 5 * b + c) for b in range(5)]
            x = [get(0, a, 5 * b + c) for b in range(5)]
            out_x, out_z = derive(z), [-v for v in derive(x)]
            oz, ox = cells.y_down(z[4]), cells.y_down(x[4])
            out_x[0] = out_x[0] - oz + penalty(x[0], ox)
            out_z[0] = out_z[0] + ox + penalty(z[0], oz)
            oz, ox = cells.y_up(z[0]), cells.y_up(x[0])
            out_x[4] = out_x[4] + oz + penalty(x[4], ox)
            out_z[4] = out_z[4] - ox + penalty(z[4], oz)
            for b in range(5):
                add(a, 5 * b + c, out_x[b], out_z[b])


def z_lines(planes, get, add, cells):
    for a in planes:
        for b in range(5):
            x = [get(0, a, 5 * b + c) for c in range(5)]
            y = [get(1, a, 5 * b + c) for c in range(5)]
            out_y, out_x = derive(x), [-v for v in derive(y)]
            ox, oy = cells.z_down(x[4]), cells.z_down(y[4])
            out_y[0] = out_y[0] - ox + penalty(y[0], oy)
            out_x[0] = out_x[0] + oy + penalty(x[0], ox)
            ox, oy = cells.z_up(x[0]), cells.z_up(y[0])
            out_y[4] = out_y[4] + ox + penalty(y[4], oy)
            out_x[4] = out_x[4] - oy + penalty(x[4], ox)
            for c in range(5):
                add(a, 5 * b + c, out_x[c], out_y[c])


def yz_into(planes, get, t, where, cells, final):
    def add_y(a, k, x, z):
        i = where(a, k)
        t[(0, *i)] = x
        t[(2, *i)] = t[(2, *i)] + z

    def add_z(a, k, x, y):
        i = where(a, k)
        final(a, k, t[(0, *i)] + x, t[(1, *i)] + y, t[(2, *i)])

    for a in planes:
        y_lines((a,), get, add_y, cells)
        z_lines((a,), get, add_z, cells)


def masks(parity, row, coef, damping):
    if parity == 1:
        m_t = rows(row, 1.0, coef, -1.0, 0.0)
        m_f = rows(row, 0.0, LIFT, -LIFT * DT, LIFT)
        m_s = rows(row, 0.0, -damping * coef, 0.0, 0.0)
    else:
        m_t = rows(row, 1.0, 0.0, 1.0, DT)
        m_f = rows(row, LIFT * coef, -LIFT, 0.0, LIFT)
        m_s = rows(row, -damping * coef, 0.0, 0.0, 0.0)
    return m_t, m_f, m_s


def materials(perm, reg, cond, aux):
    two = lambda x: jnp.concatenate([x, x, x, x], axis=0)
    perm, reg = perm[...], reg[...]
    damping = jnp.zeros((2, 128), F32)
    for r in range(8):
        damping = jnp.where(reg == r, cond[r], damping)
    coef, damping = two(DT / perm), two(damping)
    aux[0], aux[1] = coef, damping
    return coef, damping


def source_planes(step, layer, cell, amp, row, lane, coef):
    here = layer[0] == lax.axis_index("space")
    place = (row < 2) & ((row & 1) * 128 + lane == cell[0])
    shape = jnp.where(place, coef, 0.0)
    return [shape * jnp.where(here, amp[0, 3 * step + i], 0.0) for i in range(3)]


def end_traces_one(s, lo_ref, hi_ref, m_t, row):
    for k in range(25):
        for a, sign, ref in ((0, 1.0, lo_ref), (4, -1.0, hi_ref)):
            y, z = s[1, 25 * a + k] * m_t, s[2, 25 * a + k] * m_t
            ref[0, k] = jnp.where(row < 2, sign * z - swap4(y), y)
            ref[1, k] = jnp.where(row < 2, -sign * y - swap4(z), z)


def end_traces_two(sf, lo_ref, hi_ref, row):
    for k in range(25):
        for side, sign, ref in ((0, 1.0, lo_ref), (1, -1.0, hi_ref)):
            y, z = sf[1, side, k], sf[2, side, k]
            out_y = jnp.where(row < 6, swap4(y) - sign * z, DT * y)
            out_z = jnp.where(row < 6, swap4(z) + sign * y, DT * z)
            ref[0, k] = jnp.where(row < 4, ref[0, k], out_y)
            ref[1, k] = jnp.where(row < 4, ref[1, k], out_z)


def odd_ends(s, sf, tf, lo_ref, hi_ref, row, coef, damping, cells):
    m_t, m_f, m_s = masks(1, row, coef, damping)
    keep = 1.0 + m_s
    end_traces_one(s, lo_ref, hi_ref, m_t, row)
    get = lambda comp, a, k: s[comp, 25 * a + k] * m_t
    for k in range(25):
        y = [get(1, a, k) for a in range(5)]
        z = [get(2, a, k) for a in range(5)]
        dy, dz = derive_at_ends(y), derive_at_ends(z)
        for a in ENDS:
            tf[1, a // 4, k] = -dz[a] - swap4(y[a])
            tf[2, a // 4, k] = dy[a] - swap4(z[a])

    def final(a, k, *got):
        for comp in range(3):
            sf[comp, a // 4, k] = s[comp, 25 * a + k] * keep + swap4(got[comp]) * m_f

    yz_into(ENDS, get, tf, lambda a, k: (a // 4, k), cells, final)
    end_traces_two(sf, lo_ref, hi_ref, row)


def inner_kernel(s, aux, si, ci):
    row, lane = iotas()
    cells = Cells(row, lane)
    coef, damping = aux[0], aux[1]
    m_t, m_f, m_s = masks(1, row, coef, damping)
    keep = 1.0 + m_s
    get = lambda comp, a, k: s[comp, 25 * a + k] * m_t
    for k in range(25):
        dy = derive_inside([get(1, a, k) for a in range(5)])
        dz = derive_inside([get(2, a, k) for a in range(5)])
        for a in INSIDE:
            ci[1, 25 * a + k] = -dz[a]
            ci[2, 25 * a + k] = dy[a]

    def final(a, k, *got):
        for comp in range(3):
            si[comp, a - 1, k] = s[comp, 25 * a + k] * keep + swap4(got[comp]) * m_f

    whole = lambda a, k: (25 * a + k,)
    yz_into(INSIDE, get, ci, whole, cells, final)
    m_t2, _, _ = masks(2, row, coef, damping)
    get2 = lambda comp, a, k: si[comp, a - 1, k] * m_t2
    for k in range(25):
        dy = derive_from_inside([None] + [get2(1, a, k) for a in INSIDE])
        dz = derive_from_inside([None] + [get2(2, a, k) for a in INSIDE])
        for a in range(5):
            ci[1, 25 * a + k] = -dz[a]
            ci[2, 25 * a + k] = dy[a]

    def store(a, k, *got):
        for comp in range(3):
            ci[comp, 25 * a + k] = got[comp]

    yz_into(INSIDE, get2, ci, whole, cells, store)


def even_half(sf, si, ci, tf, below, above, lo_own, hi_own, row, m_t, cells, final):
    position, last = lax.axis_index("space"), lax.axis_size("space") - 1
    has = {0: (position > 0).astype(F32), 4: (position < last).astype(F32)}
    to_same = rows(row, 0.0, LIFT, 0.0, 0.0)
    to_primal = rows(row, 0.0, 0.0, LIFT * DT, 0.0)
    to_dual = rows(row, 0.0, 0.0, 0.0, LIFT)
    late_primal = rows(row, 0.0, 0.0, 1.0, 0.0)
    late_dual = rows(row, 0.0, 0.0, 0.0, 1.0)
    fix = rows(row, -LIFT * DT, LIFT * DT, 0.0, 0.0)
    for k in range(25):
        ends = {}
        for a, sign, got, own in ((0, -1.0, below, lo_own), (4, 1.0, above, hi_own)):
            y, z = got[0, k] * has[a], got[1, k] * has[a]
            ry, rz = swap4(y), swap4(z)
            s_y = sf[1, a // 4, k] + (ry * to_primal - sign * (rz * to_dual) + y * to_same)
            s_z = sf[2, a // 4, k] + (rz * to_primal + sign * (ry * to_dual) + z * to_same)
            sf[1, a // 4, k] = s_y
            sf[2, a // 4, k] = s_z
            more = has[a] * fix
            y = y + sign * swap4(own[1, k] * more)
            z = z - sign * swap4(own[0, k] * more)
            ext_y = y * late_primal - sign * (z * late_dual) + swap4(y * late_dual)
            ext_z = z * late_primal + sign * (y * late_dual) + swap4(z * late_dual)
            t_y, t_z = s_y * m_t, s_z * m_t
            ends[a] = (t_y, t_z, ext_y - swap4(t_y), ext_z - swap4(t_z))
        dy = derive_from_ends(ends[0][0], ends[4][0])
        dz = derive_from_ends(ends[0][1], ends[4][1])
        for a in range(5):
            n = 25 * a + k
            got_y, got_z = ci[1, n] - dz[a], ci[2, n] + dy[a]
            if a in ENDS:
                tf[1, a // 4, k] = got_y + ends[a][2]
                tf[2, a // 4, k] = got_z + ends[a][3]
            else:
                final(a, k, ci[0, n], got_y, got_z)
    get = lambda comp, a, k: sf[comp, a // 4, k] * m_t
    yz_into(ENDS, get, tf, lambda a, k: (a // 4, k), cells, final)


def old_plane(sf, si, comp, a, k):
    return sf[comp, a // 4, k] if a in ENDS else si[comp, a - 1, k]


def tree_sum(parts):
    while len(parts) > 1:
        parts = [sum(parts[i : i + 2]) for i in range(0, len(parts), 2)]
    return parts[0]


class Total:
    def __init__(self, zero):
        self.parts, self.turn = [zero] * 8, 0

    def add(self, x):
        self.parts[self.turn] = self.parts[self.turn] + x
        self.turn = (self.turn + 1) % 8

    def value(self):
        return tree_sum(self.parts)


def first_kernel(
    fields, cot, perm_in, reg_in, cond_in, s, sf, lo_ref, hi_ref, aux, tf, perm, reg, cond, sems
):
    row, lane = iotas()
    cells = Cells(row, lane)
    small = [
        pltpu.make_async_copy(src, dst, sems.at[4 + i])
        for i, (src, dst) in enumerate(((perm_in, perm), (reg_in, reg), (cond_in, cond)))
    ]
    copies = [
        pltpu.make_async_copy(src, s.at[:, :, pl.ds(2 * i, 2), :], sems.at[i])
        for i, src in enumerate(
            (fields.at[0:3], cot.at[0:3], fields.at[3:6], cot.at[3:6])
        )
    ]
    for copy in small + copies:
        copy.start()
    for copy in small:
        copy.wait()
    coef, damping = materials(perm, reg, cond, aux)
    for copy in copies:
        copy.wait()
    dual = (row & 2) != 0

    for a in range(5):
        for k in range(25):
            scaled = jnp.where(dual, 1.0 / node_weight(a, k), 1.0)
            for comp in range(3):
                s[comp, 25 * a + k] = s[comp, 25 * a + k] * scaled
    odd_ends(s, sf, tf, lo_ref, hi_ref, row, coef, damping, cells)


def second_kernel(
    sf_in, si, ci, lo_own, hi_own, below, above, aux, layer, cell, node_ref, amp,
    s, sf, lo_ref, hi_ref, g_ref, tf,
):
    row, lane = iotas()
    cells = Cells(row, lane)
    coef, damping = aux[0], aux[1]
    m_t, m_f, m_s = masks(2, row, coef, damping)
    total = Total(jnp.zeros((8, 128), F32))

    def final(a, k, *got):
        for comp in range(3):
            old = old_plane(sf, si, comp, a, k)
            inc = swap4(got[comp]) * m_f + old * m_s
            new = old + inc
            s[comp, 25 * a + k] = new
            total.add(pltpu.roll(inc, 2, 0) * (new * node_weight(a, k)))

    even_half(sf, si, ci, tf, below, above, lo_own, hi_own, row, m_t, cells, final)
    g = total.value()
    node = node_ref[0]
    w = weight_at(node // 25) * weight_at((node // 5) % 5) * weight_at(node % 5)
    incs = source_planes(0, layer, cell, amp, row, lane, coef)
    for comp in range(3):
        new = s[comp, node] + incs[comp]
        s[comp, node] = new
        g = g + pltpu.roll(incs[comp], 2, 0) * (new * w)
    g_ref[...] = g
    odd_ends(s, sf, tf, lo_ref, hi_ref, row, coef, damping, cells)


def third_kernel(
    sf_in, si, ci, lo_own, hi_own, below, above, aux, g_in, layer, cell, node_ref, amp, cot,
    s, g_ref, sf, tf,
):
    row, lane = iotas()
    cells = Cells(row, lane)
    coef, damping = aux[0], aux[1]
    m_t, m_f, m_s = masks(2, row, coef, damping)
    total = Total(jnp.zeros((2, 128), F32))

    def final(a, k, *got):
        for comp in range(3):
            old = old_plane(sf, si, comp, a, k)
            inc = swap4(got[comp]) * m_f + old * m_s
            s[comp, 25 * a + k] = (old + inc) * node_weight(a, k)
            total.add(inc[0:2] * cot[comp, 25 * a + k])

    even_half(sf, si, ci, tf, below, above, lo_own, hi_own, row, m_t, cells, final)
    g = total.value()
    node = node_ref[0]
    incs = source_planes(1, layer, cell, amp, row, lane, coef)
    for comp in range(3):
        g = g + incs[comp][0:2] * cot[comp, node]
    g = g + g_in[2:4]
    g_ref[...] = g * coef[0:2] * (-1.0 / DT)


def store_kernel(s, adj, sems):
    stores = [
        pltpu.make_async_copy(
            s.at[:, :, pl.ds(2 + 4 * i, 2), :], adj.at[3 * i : 3 * i + 3], sems.at[i]
        )
        for i in range(2)
    ]
    for store in stores:
        store.start()
    for store in stores:
        store.wait()


def struct(*shape):
    return jax.ShapeDtypeStruct(shape, F32)


VMEM = pl.BlockSpec(memory_space=pltpu.VMEM)
SMEM = pl.BlockSpec(memory_space=pltpu.SMEM)
HBM = pl.BlockSpec(memory_space=pltpu.HBM)
PARAMS = pltpu.CompilerParams(vmem_limit_bytes=24 * 1024 * 1024)
STATE = (3, 125, 8, 128)
FACES = (3, 2, 25, 8, 128)
INNER = (3, 3, 25, 8, 128)
TRACE = (2, 25, 8, 128)


def exchange(lo, hi):
    peers = lax.axis_size("space")
    up = [(i, (i + 1) % peers) for i in range(peers)]
    down = [((i + 1) % peers, i) for i in range(peers)]
    below = lax.ppermute(hi, "space", up)
    above = lax.ppermute(lo, "space", down)
    return below, above


def src_sum(x):
    for group in ((1, 2, 3), (4, 8, 12)):
        got = [lax.ppermute(x, "src", [(i, i ^ d) for i in range(16)]) for d in group]
        x = (x + got[0]) + (got[1] + got[2])
    return x


def on_device(
    fields, cotangent, permittivity, regions, conductance, src_layer, src_cell, src_node, src_amp
):
    wide = fields.shape[:2] + (2, 128)
    f = fields.reshape(wide)
    cot = cotangent.reshape(wide)
    perm = permittivity.reshape(2, 128)
    reg = regions.reshape(2, 128)
    f, cot, perm, reg, conductance = (
        pltpu.with_memory_space_constraint(x, pltpu.HBM) for x in (f, cot, perm, reg, conductance)
    )
    source = (src_layer, src_cell, src_node, src_amp)
    inner = pl.pallas_call(
        inner_kernel,
        out_shape=(struct(*INNER), struct(*STATE)),
        in_specs=[VMEM] * 2,
        out_specs=[VMEM] * 2,
        compiler_params=PARAMS,
        cost_estimate=pl.CostEstimate(flops=20_000_000, bytes_accessed=1000, transcendentals=0),
        name="inner",
    )
    s, sf, lo, hi, aux = pl.pallas_call(
        first_kernel,
        out_shape=(struct(*STATE), struct(*FACES), struct(*TRACE), struct(*TRACE), struct(2, 8, 128)),
        in_specs=[HBM] * 5,
        out_specs=[VMEM] * 5,
        scratch_shapes=[
            pltpu.VMEM(FACES, F32),
            pltpu.VMEM((2, 128), F32),
            pltpu.VMEM((2, 128), jnp.int32),
            pltpu.SMEM((8,), F32),
            pltpu.SemaphoreType.DMA((7,)),
        ],
        compiler_params=PARAMS,
        name="first",
    )(f, cot, perm, reg, conductance)
    below, above = exchange(lo, hi)
    si, ci = inner(s, aux)
    s, sf, lo, hi, g = pl.pallas_call(
        second_kernel,
        out_shape=(struct(*STATE), struct(*FACES), struct(*TRACE), struct(*TRACE), struct(8, 128)),
        in_specs=[VMEM] * 8 + [SMEM] * 4,
        out_specs=[VMEM] * 5,
        input_output_aliases={0: 1},
        scratch_shapes=[pltpu.VMEM(FACES, F32)],
        compiler_params=PARAMS,
        name="second",
    )(sf, si, ci, lo, hi, below, above, aux, *source)
    below, above = exchange(lo, hi)
    si, ci = inner(s, aux)
    s, g, _ = pl.pallas_call(
        third_kernel,
        out_shape=(struct(*STATE), struct(2, 128), struct(*FACES)),
        in_specs=[VMEM] * 9 + [SMEM] * 4 + [VMEM],
        out_specs=[VMEM] * 3,
        input_output_aliases={0: 2},
        scratch_shapes=[pltpu.VMEM(FACES, F32)],
        compiler_params=PARAMS,
        name="third",
    )(sf, si, ci, lo, hi, below, above, aux, g, *source, cotangent.reshape(wide))
    adjoint = pl.pallas_call(
        store_kernel,
        out_shape=struct(*wide),
        in_specs=[VMEM],
        out_specs=HBM,
        scratch_shapes=[pltpu.SemaphoreType.DMA((2,))],
        compiler_params=PARAMS,
        cost_estimate=pl.CostEstimate(flops=0, bytes_accessed=4_000_000, transcendentals=0),
        name="store",
    )(s)
    gradient = src_sum(g).reshape(permittivity.shape)
    adjoint = with_layout_constraint(adjoint.reshape(fields.shape), Layout((0, 1, 2, 3, 4)))
    return adjoint, gradient


def solution(mesh):
    return jax.shard_map(
        on_device,
        mesh=mesh,
        in_specs=(
            P(None, None, "src", "space", None),
            P(None, None, "src", "space", None),
            P("space", None),
            P("space", None),
            P(),
            P("src"),
            P("src"),
            P("src"),
            P("src", None),
        ),
        out_specs=(P(None, None, "src", "space", None), P("space", None)),
        check_vma=False,
    )
```

```python
import math

import jax
import jax.numpy as jnp
import numpy as np
from jax import lax
from jax.experimental import pallas as pl
from jax.experimental.layout import Layout, with_layout_constraint
from jax.experimental.pallas import tpu as pltpu
from jax.sharding import PartitionSpec as P

EZ = 16
DT = 0.02
LIFT = 10.0
METRIC = 2.0
F32 = jnp.float32


WEIGHTS = (1.0 / 10.0, 49.0 / 90.0, 32.0 / 45.0, 49.0 / 90.0, 1.0 / 10.0)


def central_matrix():
    points = np.array([-1.0, -math.sqrt(3.0 / 7.0), 0.0, math.sqrt(3.0 / 7.0), 1.0])
    products = [
        np.prod([points[i] - points[j] for j in range(5) if j != i]) for i in range(5)
    ]
    matrix = np.zeros((5, 5))
    for i in range(5):
        for j in range(5):
            if j != i:
                matrix[i, j] = products[i] / (products[j] * (points[i] - points[j]))
    for i in range(5):
        matrix[i, i] = -np.sum(matrix[i])
    return (METRIC * matrix + np.diag([LIFT, 0.0, 0.0, 0.0, -LIFT])) / LIFT


CENTRAL = central_matrix()


def halves():
    d = CENTRAL
    h = [[float(0.5 * (d[i, j] - d[i, 4 - j])) for j in range(2)] for i in range(2)]
    g = [[float(0.5 * (d[i, j] + d[i, 4 - j])) for j in range(2)] for i in range(2)]
    return h, g, [float(d[i, 2]) for i in range(2)], [float(d[2, j]) for j in range(2)]


ODD, EVEN, MIDDLE, CENTRE = halves()


def derive(u):
    e0, e1, m = u[0] + u[4], u[1] + u[3], u[2]
    o0, o1 = u[0] - u[4], u[1] - u[3]
    s0 = ODD[0][0] * o0 + ODD[0][1] * o1
    s1 = ODD[1][0] * o0 + ODD[1][1] * o1
    d0 = EVEN[0][0] * e0 + EVEN[0][1] * e1 + MIDDLE[0] * m
    d1 = EVEN[1][0] * e0 + EVEN[1][1] * e1 + MIDDLE[1] * m
    mid = CENTRE[0] * o0 + CENTRE[1] * o1
    return [s0 + d0, s1 + d1, mid, s1 - d1, s0 - d0]


def derive_at_ends(u):
    e0, e1, m = u[0] + u[4], u[1] + u[3], u[2]
    o0, o1 = u[0] - u[4], u[1] - u[3]
    s0 = ODD[0][0] * o0 + ODD[0][1] * o1
    d0 = EVEN[0][0] * e0 + EVEN[0][1] * e1 + MIDDLE[0] * m
    return {0: s0 + d0, 4: s0 - d0}


def derive_inside(u):
    e0, e1, m = u[0] + u[4], u[1] + u[3], u[2]
    o0, o1 = u[0] - u[4], u[1] - u[3]
    s1 = ODD[1][0] * o0 + ODD[1][1] * o1
    d1 = EVEN[1][0] * e0 + EVEN[1][1] * e1 + MIDDLE[1] * m
    mid = CENTRE[0] * o0 + CENTRE[1] * o1
    return {1: s1 + d1, 2: mid, 3: s1 - d1}


def derive_from_inside(u):
    e1, o1, m = u[1] + u[3], u[1] - u[3], u[2]
    s0, s1 = ODD[0][1] * o1, ODD[1][1] * o1
    d0 = EVEN[0][1] * e1 + MIDDLE[0] * m
    d1 = EVEN[1][1] * e1 + MIDDLE[1] * m
    return [s0 + d0, s1 + d1, CENTRE[1] * o1, s1 - d1, s0 - d0]


def derive_from_ends(u0, u4):
    e0, o0 = u0 + u4, u0 - u4
    s0, s1 = ODD[0][0] * o0, ODD[1][0] * o0
    d0, d1 = EVEN[0][0] * e0, EVEN[1][0] * e0
    return [s0 + d0, s1 + d1, CENTRE[0] * o0, s1 - d1, s0 - d0]


def swap4(x):
    return pltpu.roll(x, 4, 0)


def iotas():
    row = lax.broadcasted_iota(jnp.int32, (8, 128), 0)
    lane = lax.broadcasted_iota(jnp.int32, (8, 128), 1)
    return row, lane


def rows(row, v0, v1, v2, v3):
    return jnp.where(row < 2, v0, jnp.where(row < 4, v1, jnp.where(row < 6, v2, v3)))


class Cells:
    def __init__(self, row, lane):
        self.even = (row & 1) == 0
        self.y_last = lane >= 112
        self.y_first = lane < 16
        self.z_last = (lane & 15) == 15
        self.z_first = (lane & 15) == 0

    def other_half(self, x):
        return jnp.where(self.even, pltpu.roll(x, 7, 0), pltpu.roll(x, 1, 0))

    def y_up(self, x):
        x = pltpu.roll(x, 112, 1)
        return jnp.where(self.y_last, self.other_half(x), x)

    def y_down(self, x):
        x = pltpu.roll(x, 16, 1)
        return jnp.where(self.y_first, self.other_half(x), x)

    def z_up(self, x):
        return jnp.where(self.z_last, pltpu.roll(x, 15, 1), pltpu.roll(x, 127, 1))

    def z_down(self, x):
        return jnp.where(self.z_first, pltpu.roll(x, 113, 1), pltpu.roll(x, 1, 1))


ENDS, INSIDE = (0, 4), (1, 2, 3)


def node_weight(a, k):
    return WEIGHTS[a] * WEIGHTS[k // 5] * WEIGHTS[k % 5]


def weight_at(i):
    return jnp.where((i == 0) | (i == 4), WEIGHTS[0], jnp.where(i == 2, WEIGHTS[2], WEIGHTS[1]))


def penalty(inner, outer):
    return swap4(outer - inner)


def y_lines(planes, get, add, cells):
    for a in planes:
        for c in range(5):
            z = [get(2, a, 5 * b + c) for b in range(5)]
            x = [get(0, a, 5 * b + c) for b in range(5)]
            out_x, out_z = derive(z), [-v for v in derive(x)]
            oz, ox = cells.y_down(z[4]), cells.y_down(x[4])
            out_x[0] = out_x[0] - oz + penalty(x[0], ox)
            out_z[0] = out_z[0] + ox + penalty(z[0], oz)
            oz, ox = cells.y_up(z[0]), cells.y_up(x[0])
            out_x[4] = out_x[4] + oz + penalty(x[4], ox)
            out_z[4] = out_z[4] - ox + penalty(z[4], oz)
            for b in range(5):
                add(a, 5 * b + c, out_x[b], out_z[b])


def z_lines(planes, get, add, cells):
    for a in planes:
        for b in range(5):
            x = [get(0, a, 5 * b + c) for c in range(5)]
            y = [get(1, a, 5 * b + c) for c in range(5)]
            out_y, out_x = derive(x), [-v for v in derive(y)]
            ox, oy = cells.z_down(x[4]), cells.z_down(y[4])
            out_y[0] = out_y[0] - ox + penalty(y[0], oy)
            out_x[0] = out_x[0] + oy + penalty(x[0], ox)
            ox, oy = cells.z_up(x[0]), cells.z_up(y[0])
            out_y[4] = out_y[4] + ox + penalty(y[4], oy)
            out_x[4] = out_x[4] - oy + penalty(x[4], ox)
            for c in range(5):
                add(a, 5 * b + c, out_x[c], out_y[c])


def yz_into(planes, get, t, where, cells, final):
    def add_y(a, k, x, z):
        i = where(a, k)
        t[(0, *i)] = x
        t[(2, *i)] = t[(2, *i)] + z

    def add_z(a, k, x, y):
        i = where(a, k)
        final(a, k, t[(0, *i)] + x, t[(1, *i)] + y, t[(2, *i)])

    for a in planes:
        y_lines((a,), get, add_y, cells)
        z_lines((a,), get, add_z, cells)


def masks(parity, row, coef, damping):
    if parity == 1:
        m_t = rows(row, 1.0, coef, -1.0, 0.0)
        m_f = rows(row, 0.0, LIFT, -LIFT * DT, LIFT)
        m_s = rows(row, 0.0, -damping * coef, 0.0, 0.0)
    else:
        m_t = rows(row, 1.0, 0.0, 1.0, DT)
        m_f = rows(row, LIFT * coef, -LIFT, 0.0, LIFT)
        m_s = rows(row, -damping * coef, 0.0, 0.0, 0.0)
    return m_t, m_f, m_s


def materials(perm, reg, cond, aux):
    two = lambda x: jnp.concatenate([x, x, x, x], axis=0)
    perm, reg = perm[...], reg[...]
    damping = jnp.zeros((2, 128), F32)
    for r in range(8):
        damping = jnp.where(reg == r, cond[r], damping)
    coef, damping = two(DT / perm), two(damping)
    aux[0], aux[1] = coef, damping
    return coef, damping


def source_planes(step, layer, cell, amp, row, lane, coef):
    here = layer[0] == lax.axis_index("space")
    place = (row < 2) & ((row & 1) * 128 + lane == cell[0])
    shape = jnp.where(place, coef, 0.0)
    return [shape * jnp.where(here, amp[0, 3 * step + i], 0.0) for i in range(3)]


def end_traces_one(s, lo_ref, hi_ref, m_t, row):
    for k in range(25):
        for a, sign, ref in ((0, 1.0, lo_ref), (4, -1.0, hi_ref)):
            y, z = s[1, 25 * a + k] * m_t, s[2, 25 * a + k] * m_t
            ref[0, k] = jnp.where(row < 2, sign * z - swap4(y), y)
            ref[1, k] = jnp.where(row < 2, -sign * y - swap4(z), z)


def end_traces_two(sf, lo_ref, hi_ref, row):
    for k in range(25):
        for side, sign, ref in ((0, 1.0, lo_ref), (1, -1.0, hi_ref)):
            y, z = sf[1, side, k], sf[2, side, k]
            out_y = jnp.where(row < 6, swap4(y) - sign * z, DT * y)
            out_z = jnp.where(row < 6, swap4(z) + sign * y, DT * z)
            ref[0, k] = jnp.where(row < 4, ref[0, k], out_y)
            ref[1, k] = jnp.where(row < 4, ref[1, k], out_z)


def odd_ends(s, sf, tf, lo_ref, hi_ref, row, coef, damping, cells):
    m_t, m_f, m_s = masks(1, row, coef, damping)
    keep = 1.0 + m_s
    end_traces_one(s, lo_ref, hi_ref, m_t, row)
    get = lambda comp, a, k: s[comp, 25 * a + k] * m_t
    for k in range(25):
        y = [get(1, a, k) for a in range(5)]
        z = [get(2, a, k) for a in range(5)]
        dy, dz = derive_at_ends(y), derive_at_ends(z)
        for a in ENDS:
            tf[1, a // 4, k] = -dz[a] - swap4(y[a])
            tf[2, a // 4, k] = dy[a] - swap4(z[a])

    def final(a, k, *got):
        for comp in range(3):
            sf[comp, a // 4, k] = s[comp, 25 * a + k] * keep + swap4(got[comp]) * m_f

    yz_into(ENDS, get, tf, lambda a, k: (a // 4, k), cells, final)
    end_traces_two(sf, lo_ref, hi_ref, row)


def inner_kernel(s, aux, si, ci):
    row, lane = iotas()
    cells = Cells(row, lane)
    coef, damping = aux[0], aux[1]
    m_t, m_f, m_s = masks(1, row, coef, damping)
    keep = 1.0 + m_s
    get = lambda comp, a, k: s[comp, 25 * a + k] * m_t
    for k in range(25):
        dy = derive_inside([get(1, a, k) for a in range(5)])
        dz = derive_inside([get(2, a, k) for a in range(5)])
        for a in INSIDE:
            ci[1, 25 * a + k] = -dz[a]
            ci[2, 25 * a + k] = dy[a]

    def final(a, k, *got):
        for comp in range(3):
            si[comp, a - 1, k] = s[comp, 25 * a + k] * keep + swap4(got[comp]) * m_f

    whole = lambda a, k: (25 * a + k,)
    yz_into(INSIDE, get, ci, whole, cells, final)
    m_t2, _, _ = masks(2, row, coef, damping)
    get2 = lambda comp, a, k: si[comp, a - 1, k] * m_t2
    for k in range(25):
        dy = derive_from_inside([None] + [get2(1, a, k) for a in INSIDE])
        dz = derive_from_inside([None] + [get2(2, a, k) for a in INSIDE])
        for a in range(5):
            ci[1, 25 * a + k] = -dz[a]
            ci[2, 25 * a + k] = dy[a]

    def store(a, k, *got):
        for comp in range(3):
            ci[comp, 25 * a + k] = got[comp]

    yz_into(INSIDE, get2, ci, whole, cells, store)


def even_half(sf, si, ci, tf, below, above, lo_own, hi_own, row, m_t, cells, final):
    position, last = lax.axis_index("space"), lax.axis_size("space") - 1
    has = {0: (position > 0).astype(F32), 4: (position < last).astype(F32)}
    to_same = rows(row, 0.0, LIFT, 0.0, 0.0)
    to_primal = rows(row, 0.0, 0.0, LIFT * DT, 0.0)
    to_dual = rows(row, 0.0, 0.0, 0.0, LIFT)
    late_primal = rows(row, 0.0, 0.0, 1.0, 0.0)
    late_dual = rows(row, 0.0, 0.0, 0.0, 1.0)
    fix = rows(row, -LIFT * DT, LIFT * DT, 0.0, 0.0)
    for k in range(25):
        ends = {}
        for a, sign, got, own in ((0, -1.0, below, lo_own), (4, 1.0, above, hi_own)):
            y, z = got[0, k] * has[a], got[1, k] * has[a]
            ry, rz = swap4(y), swap4(z)
            s_y = sf[1, a // 4, k] + (ry * to_primal - sign * (rz * to_dual) + y * to_same)
            s_z = sf[2, a // 4, k] + (rz * to_primal + sign * (ry * to_dual) + z * to_same)
            sf[1, a // 4, k] = s_y
            sf[2, a // 4, k] = s_z
            more = has[a] * fix
            y = y + sign * swap4(own[1, k] * more)
            z = z - sign * swap4(own[0, k] * more)
            ext_y = y * late_primal - sign * (z * late_dual) + swap4(y * late_dual)
            ext_z = z * late_primal + sign * (y * late_dual) + swap4(z * late_dual)
            t_y, t_z = s_y * m_t, s_z * m_t
            ends[a] = (t_y, t_z, ext_y - swap4(t_y), ext_z - swap4(t_z))
        dy = derive_from_ends(ends[0][0], ends[4][0])
        dz = derive_from_ends(ends[0][1], ends[4][1])
        for a in range(5):
            n = 25 * a + k
            got_y, got_z = ci[1, n] - dz[a], ci[2, n] + dy[a]
            if a in ENDS:
                tf[1, a // 4, k] = got_y + ends[a][2]
                tf[2, a // 4, k] = got_z + ends[a][3]
            else:
                final(a, k, ci[0, n], got_y, got_z)
    get = lambda comp, a, k: sf[comp, a // 4, k] * m_t
    yz_into(ENDS, get, tf, lambda a, k: (a // 4, k), cells, final)


def old_plane(sf, si, comp, a, k):
    return sf[comp, a // 4, k] if a in ENDS else si[comp, a - 1, k]


def tree_sum(parts):
    while len(parts) > 1:
        parts = [sum(parts[i : i + 2]) for i in range(0, len(parts), 2)]
    return parts[0]


class Total:
    def __init__(self, zero):
        self.parts, self.turn = [zero] * 8, 0

    def add(self, x):
        self.parts[self.turn] = self.parts[self.turn] + x
        self.turn = (self.turn + 1) % 8

    def value(self):
        return tree_sum(self.parts)


def first_kernel(
    fields, cot, perm_in, reg_in, cond_in, s, sf, lo_ref, hi_ref, aux, tf, perm, reg, cond, sems
):
    row, lane = iotas()
    cells = Cells(row, lane)
    small = [
        pltpu.make_async_copy(src, dst, sems.at[4 + i])
        for i, (src, dst) in enumerate(((perm_in, perm), (reg_in, reg), (cond_in, cond)))
    ]
    copies = [
        pltpu.make_async_copy(src, s.at[:, :, pl.ds(2 * i, 2), :], sems.at[i])
        for i, src in enumerate(
            (fields.at[0:3], cot.at[0:3], fields.at[3:6], cot.at[3:6])
        )
    ]
    for copy in small + copies:
        copy.start()
    for copy in small:
        copy.wait()
    coef, damping = materials(perm, reg, cond, aux)
    for copy in copies:
        copy.wait()
    dual = (row & 2) != 0

    for a in range(5):
        for k in range(25):
            scaled = jnp.where(dual, 1.0 / node_weight(a, k), 1.0)
            for comp in range(3):
                s[comp, 25 * a + k] = s[comp, 25 * a + k] * scaled
    odd_ends(s, sf, tf, lo_ref, hi_ref, row, coef, damping, cells)


def second_kernel(
    sf_in, si, ci, lo_own, hi_own, below, above, aux, layer, cell, node_ref, amp,
    s, sf, lo_ref, hi_ref, g_ref, tf,
):
    row, lane = iotas()
    cells = Cells(row, lane)
    coef, damping = aux[0], aux[1]
    m_t, m_f, m_s = masks(2, row, coef, damping)
    total = Total(jnp.zeros((8, 128), F32))

    def final(a, k, *got):
        for comp in range(3):
            old = old_plane(sf, si, comp, a, k)
            inc = swap4(got[comp]) * m_f + old * m_s
            new = old + inc
            s[comp, 25 * a + k] = new
            total.add(pltpu.roll(inc, 2, 0) * (new * node_weight(a, k)))

    even_half(sf, si, ci, tf, below, above, lo_own, hi_own, row, m_t, cells, final)
    g = total.value()
    node = node_ref[0]
    w = weight_at(node // 25) * weight_at((node // 5) % 5) * weight_at(node % 5)
    incs = source_planes(0, layer, cell, amp, row, lane, coef)
    for comp in range(3):
        new = s[comp, node] + incs[comp]
        s[comp, node] = new
        g = g + pltpu.roll(incs[comp], 2, 0) * (new * w)
    g_ref[...] = g
    odd_ends(s, sf, tf, lo_ref, hi_ref, row, coef, damping, cells)


def third_kernel(
    sf_in, si, ci, lo_own, hi_own, below, above, aux, g_in, layer, cell, node_ref, amp, cot,
    s, g_ref, sf, tf,
):
    row, lane = iotas()
    cells = Cells(row, lane)
    coef, damping = aux[0], aux[1]
    m_t, m_f, m_s = masks(2, row, coef, damping)
    total = Total(jnp.zeros((2, 128), F32))

    def final(a, k, *got):
        for comp in range(3):
            old = old_plane(sf, si, comp, a, k)
            inc = swap4(got[comp]) * m_f + old * m_s
            s[comp, 25 * a + k] = (old + inc) * node_weight(a, k)
            total.add(inc[0:2] * cot[comp, 25 * a + k])

    even_half(sf, si, ci, tf, below, above, lo_own, hi_own, row, m_t, cells, final)
    g = total.value()
    node = node_ref[0]
    incs = source_planes(1, layer, cell, amp, row, lane, coef)
    for comp in range(3):
        g = g + incs[comp][0:2] * cot[comp, node]
    g = g + g_in[2:4]
    g_ref[...] = g * coef[0:2] * (-1.0 / DT)


def store_kernel(s, adj, sems):
    stores = [
        pltpu.make_async_copy(
            s.at[:, :, pl.ds(2 + 4 * i, 2), :], adj.at[3 * i : 3 * i + 3], sems.at[i]
        )
        for i in range(2)
    ]
    for store in stores:
        store.start()
    for store in stores:
        store.wait()


def struct(*shape):
    return jax.ShapeDtypeStruct(shape, F32)


VMEM = pl.BlockSpec(memory_space=pltpu.VMEM)
SMEM = pl.BlockSpec(memory_space=pltpu.SMEM)
HBM = pl.BlockSpec(memory_space=pltpu.HBM)
PARAMS = pltpu.CompilerParams(vmem_limit_bytes=24 * 1024 * 1024)
STATE = (3, 125, 8, 128)
FACES = (3, 2, 25, 8, 128)
INNER = (3, 3, 25, 8, 128)
TRACE = (2, 25, 8, 128)


def exchange(lo, hi):
    peers = lax.axis_size("space")
    even = lax.axis_index("space") % 2 == 0
    inner_pairs = [(i, i ^ 1) for i in range(peers)]
    outer_pairs = [(i, (i + 2 * (i % 2) - 1) % peers) for i in range(peers)]
    one, two = lax.optimization_barrier((jnp.where(even, lo, hi), jnp.where(even, hi, lo)))
    got_one = lax.ppermute(one, "space", outer_pairs)
    got_two = lax.ppermute(two, "space", inner_pairs)
    return jnp.where(even, got_one, got_two), jnp.where(even, got_two, got_one)


def src_sum(x):
    for group in ((1, 2, 3), (4, 8, 12)):
        got = [lax.ppermute(x, "src", [(i, i ^ d) for i in range(16)]) for d in group]
        x = (x + got[0]) + (got[1] + got[2])
    return x


def on_device(
    fields, cotangent, permittivity, regions, conductance, src_layer, src_cell, src_node, src_amp
):
    wide = fields.shape[:2] + (2, 128)
    f = fields.reshape(wide)
    cot = cotangent.reshape(wide)
    perm = permittivity.reshape(2, 128)
    reg = regions.reshape(2, 128)
    f, cot, perm, reg, conductance = (
        pltpu.with_memory_space_constraint(x, pltpu.HBM) for x in (f, cot, perm, reg, conductance)
    )
    source = (src_layer, src_cell, src_node, src_amp)
    inner = pl.pallas_call(
        inner_kernel,
        out_shape=(struct(*INNER), struct(*STATE)),
        in_specs=[VMEM] * 2,
        out_specs=[VMEM] * 2,
        compiler_params=PARAMS,
        cost_estimate=pl.CostEstimate(flops=20_000_000, bytes_accessed=1000, transcendentals=0),
        name="inner",
    )
    s, sf, lo, hi, aux = pl.pallas_call(
        first_kernel,
        out_shape=(struct(*STATE), struct(*FACES), struct(*TRACE), struct(*TRACE), struct(2, 8, 128)),
        in_specs=[HBM] * 5,
        out_specs=[VMEM] * 5,
        scratch_shapes=[
            pltpu.VMEM(FACES, F32),
            pltpu.VMEM((2, 128), F32),
            pltpu.VMEM((2, 128), jnp.int32),
            pltpu.SMEM((8,), F32),
            pltpu.SemaphoreType.DMA((7,)),
        ],
        compiler_params=PARAMS,
        name="first",
    )(f, cot, perm, reg, conductance)
    below, above = exchange(lo, hi)
    si, ci = inner(s, aux)
    s, sf, lo, hi, g = pl.pallas_call(
        second_kernel,
        out_shape=(struct(*STATE), struct(*FACES), struct(*TRACE), struct(*TRACE), struct(8, 128)),
        in_specs=[VMEM] * 8 + [SMEM] * 4,
        out_specs=[VMEM] * 5,
        input_output_aliases={0: 1},
        scratch_shapes=[pltpu.VMEM(FACES, F32)],
        compiler_params=PARAMS,
        name="second",
    )(sf, si, ci, lo, hi, below, above, aux, *source)
    below, above = exchange(lo, hi)
    si, ci = inner(s, aux)
    s, g, _ = pl.pallas_call(
        third_kernel,
        out_shape=(struct(*STATE), struct(2, 128), struct(*FACES)),
        in_specs=[VMEM] * 9 + [SMEM] * 4 + [VMEM],
        out_specs=[VMEM] * 3,
        input_output_aliases={0: 2},
        scratch_shapes=[pltpu.VMEM(FACES, F32)],
        compiler_params=PARAMS,
        name="third",
    )(sf, si, ci, lo, hi, below, above, aux, g, *source, cotangent.reshape(wide))
    adjoint = pl.pallas_call(
        store_kernel,
        out_shape=struct(*wide),
        in_specs=[VMEM],
        out_specs=HBM,
        scratch_shapes=[pltpu.SemaphoreType.DMA((2,))],
        compiler_params=PARAMS,
        cost_estimate=pl.CostEstimate(flops=0, bytes_accessed=4_000_000, transcendentals=0),
        name="store",
    )(s)
    gradient = src_sum(g).reshape(permittivity.shape)
    adjoint = with_layout_constraint(adjoint.reshape(fields.shape), Layout((0, 1, 2, 3, 4)))
    return adjoint, gradient


def solution(mesh):
    return jax.shard_map(
        on_device,
        mesh=mesh,
        in_specs=(
            P(None, None, "src", "space", None),
            P(None, None, "src", "space", None),
            P("space", None),
            P("space", None),
            P(),
            P("src"),
            P("src"),
            P("src"),
            P("src", None),
        ),
        out_specs=(P(None, None, "src", "space", None), P("space", None)),
        check_vma=False,
    )
```

```python
import math

import jax
import jax.numpy as jnp
import numpy as np
from jax import lax
from jax.experimental import pallas as pl
from jax.experimental.layout import Layout, with_layout_constraint
from jax.experimental.pallas import tpu as pltpu
from jax.sharding import PartitionSpec as P

EZ = 16
DT = 0.02
LIFT = 10.0
METRIC = 2.0
F32 = jnp.float32


WEIGHTS = (1.0 / 10.0, 49.0 / 90.0, 32.0 / 45.0, 49.0 / 90.0, 1.0 / 10.0)


def central_matrix():
    points = np.array([-1.0, -math.sqrt(3.0 / 7.0), 0.0, math.sqrt(3.0 / 7.0), 1.0])
    products = [
        np.prod([points[i] - points[j] for j in range(5) if j != i]) for i in range(5)
    ]
    matrix = np.zeros((5, 5))
    for i in range(5):
        for j in range(5):
            if j != i:
                matrix[i, j] = products[i] / (products[j] * (points[i] - points[j]))
    for i in range(5):
        matrix[i, i] = -np.sum(matrix[i])
    return (METRIC * matrix + np.diag([LIFT, 0.0, 0.0, 0.0, -LIFT])) / LIFT


CENTRAL = central_matrix()


def halves():
    d = CENTRAL
    h = [[float(0.5 * (d[i, j] - d[i, 4 - j])) for j in range(2)] for i in range(2)]
    g = [[float(0.5 * (d[i, j] + d[i, 4 - j])) for j in range(2)] for i in range(2)]
    return h, g, [float(d[i, 2]) for i in range(2)], [float(d[2, j]) for j in range(2)]


ODD, EVEN, MIDDLE, CENTRE = halves()


def derive(u):
    e0, e1, m = u[0] + u[4], u[1] + u[3], u[2]
    o0, o1 = u[0] - u[4], u[1] - u[3]
    s0 = ODD[0][0] * o0 + ODD[0][1] * o1
    s1 = ODD[1][0] * o0 + ODD[1][1] * o1
    d0 = EVEN[0][0] * e0 + EVEN[0][1] * e1 + MIDDLE[0] * m
    d1 = EVEN[1][0] * e0 + EVEN[1][1] * e1 + MIDDLE[1] * m
    mid = CENTRE[0] * o0 + CENTRE[1] * o1
    return [s0 + d0, s1 + d1, mid, s1 - d1, s0 - d0]


def derive_at_ends(u):
    e0, e1, m = u[0] + u[4], u[1] + u[3], u[2]
    o0, o1 = u[0] - u[4], u[1] - u[3]
    s0 = ODD[0][0] * o0 + ODD[0][1] * o1
    d0 = EVEN[0][0] * e0 + EVEN[0][1] * e1 + MIDDLE[0] * m
    return {0: s0 + d0, 4: s0 - d0}


def derive_inside(u):
    e0, e1, m = u[0] + u[4], u[1] + u[3], u[2]
    o0, o1 = u[0] - u[4], u[1] - u[3]
    s1 = ODD[1][0] * o0 + ODD[1][1] * o1
    d1 = EVEN[1][0] * e0 + EVEN[1][1] * e1 + MIDDLE[1] * m
    mid = CENTRE[0] * o0 + CENTRE[1] * o1
    return {1: s1 + d1, 2: mid, 3: s1 - d1}


def derive_from_inside(u):
    e1, o1, m = u[1] + u[3], u[1] - u[3], u[2]
    s0, s1 = ODD[0][1] * o1, ODD[1][1] * o1
    d0 = EVEN[0][1] * e1 + MIDDLE[0] * m
    d1 = EVEN[1][1] * e1 + MIDDLE[1] * m
    return [s0 + d0, s1 + d1, CENTRE[1] * o1, s1 - d1, s0 - d0]


def derive_from_ends(u0, u4):
    e0, o0 = u0 + u4, u0 - u4
    s0, s1 = ODD[0][0] * o0, ODD[1][0] * o0
    d0, d1 = EVEN[0][0] * e0, EVEN[1][0] * e0
    return [s0 + d0, s1 + d1, CENTRE[0] * o0, s1 - d1, s0 - d0]


def swap4(x):
    return pltpu.roll(x, 4, 0)


def iotas():
    row = lax.broadcasted_iota(jnp.int32, (8, 128), 0)
    lane = lax.broadcasted_iota(jnp.int32, (8, 128), 1)
    return row, lane


def rows(row, v0, v1, v2, v3):
    return jnp.where(row < 2, v0, jnp.where(row < 4, v1, jnp.where(row < 6, v2, v3)))


class Cells:
    def __init__(self, row, lane):
        self.even = (row & 1) == 0
        self.y_last = lane >= 112
        self.y_first = lane < 16
        self.z_last = (lane & 15) == 15
        self.z_first = (lane & 15) == 0

    def other_half(self, x):
        return jnp.where(self.even, pltpu.roll(x, 7, 0), pltpu.roll(x, 1, 0))

    def y_up(self, x):
        x = pltpu.roll(x, 112, 1)
        return jnp.where(self.y_last, self.other_half(x), x)

    def y_down(self, x):
        x = pltpu.roll(x, 16, 1)
        return jnp.where(self.y_first, self.other_half(x), x)

    def z_up(self, x):
        return jnp.where(self.z_last, pltpu.roll(x, 15, 1), pltpu.roll(x, 127, 1))

    def z_down(self, x):
        return jnp.where(self.z_first, pltpu.roll(x, 113, 1), pltpu.roll(x, 1, 1))


ENDS, INSIDE = (0, 4), (1, 2, 3)


def node_weight(a, k):
    return WEIGHTS[a] * WEIGHTS[k // 5] * WEIGHTS[k % 5]


def weight_at(i):
    return jnp.where((i == 0) | (i == 4), WEIGHTS[0], jnp.where(i == 2, WEIGHTS[2], WEIGHTS[1]))


def penalty(inner, outer):
    return swap4(outer - inner)


def y_lines(planes, get, add, cells):
    for a in planes:
        for c in range(5):
            z = [get(2, a, 5 * b + c) for b in range(5)]
            x = [get(0, a, 5 * b + c) for b in range(5)]
            out_x, out_z = derive(z), [-v for v in derive(x)]
            oz, ox = cells.y_down(z[4]), cells.y_down(x[4])
            out_x[0] = out_x[0] - oz + penalty(x[0], ox)
            out_z[0] = out_z[0] + ox + penalty(z[0], oz)
            oz, ox = cells.y_up(z[0]), cells.y_up(x[0])
            out_x[4] = out_x[4] + oz + penalty(x[4], ox)
            out_z[4] = out_z[4] - ox + penalty(z[4], oz)
            for b in range(5):
                add(a, 5 * b + c, out_x[b], out_z[b])


def z_lines(planes, get, add, cells):
    for a in planes:
        for b in range(5):
            x = [get(0, a, 5 * b + c) for c in range(5)]
            y = [get(1, a, 5 * b + c) for c in range(5)]
            out_y, out_x = derive(x), [-v for v in derive(y)]
            ox, oy = cells.z_down(x[4]), cells.z_down(y[4])
            out_y[0] = out_y[0] - ox + penalty(y[0], oy)
            out_x[0] = out_x[0] + oy + penalty(x[0], ox)
            ox, oy = cells.z_up(x[0]), cells.z_up(y[0])
            out_y[4] = out_y[4] + ox + penalty(y[4], oy)
            out_x[4] = out_x[4] - oy + penalty(x[4], ox)
            for c in range(5):
                add(a, 5 * b + c, out_x[c], out_y[c])


def yz_into(planes, get, t, where, cells, final):
    def add_y(a, k, x, z):
        i = where(a, k)
        t[(0, *i)] = x
        t[(2, *i)] = t[(2, *i)] + z

    def add_z(a, k, x, y):
        i = where(a, k)
        final(a, k, t[(0, *i)] + x, t[(1, *i)] + y, t[(2, *i)])

    for a in planes:
        y_lines((a,), get, add_y, cells)
        z_lines((a,), get, add_z, cells)


def masks(parity, row, coef, damping):
    if parity == 1:
        m_t = rows(row, 1.0, coef, -1.0, 0.0)
        m_f = rows(row, 0.0, LIFT, -LIFT * DT, LIFT)
        m_s = rows(row, 0.0, -damping * coef, 0.0, 0.0)
    else:
        m_t = rows(row, 1.0, 0.0, 1.0, DT)
        m_f = rows(row, LIFT * coef, -LIFT, 0.0, LIFT)
        m_s = rows(row, -damping * coef, 0.0, 0.0, 0.0)
    return m_t, m_f, m_s


def materials(perm, reg, cond, aux):
    two = lambda x: jnp.concatenate([x, x, x, x], axis=0)
    perm, reg = perm[...], reg[...]
    damping = jnp.zeros((2, 128), F32)
    for r in range(8):
        damping = jnp.where(reg == r, cond[r], damping)
    coef, damping = two(DT / perm), two(damping)
    aux[0], aux[1] = coef, damping
    return coef, damping


def source_planes(step, layer, cell, amp, row, lane, coef):
    here = layer[0] == lax.axis_index("space")
    place = (row < 2) & ((row & 1) * 128 + lane == cell[0])
    shape = jnp.where(place, coef, 0.0)
    return [shape * jnp.where(here, amp[0, 3 * step + i], 0.0) for i in range(3)]


def end_traces_one(s, lo_ref, hi_ref, m_t, row):
    for k in range(25):
        for a, sign, ref in ((0, 1.0, lo_ref), (4, -1.0, hi_ref)):
            y, z = s[1, 25 * a + k] * m_t, s[2, 25 * a + k] * m_t
            ref[0, k] = jnp.where(row < 2, sign * z - swap4(y), y)
            ref[1, k] = jnp.where(row < 2, -sign * y - swap4(z), z)


def end_traces_two(sf, lo_ref, hi_ref, row):
    for k in range(25):
        for side, sign, ref in ((0, 1.0, lo_ref), (1, -1.0, hi_ref)):
            y, z = sf[1, side, k], sf[2, side, k]
            out_y = jnp.where(row < 6, swap4(y) - sign * z, DT * y)
            out_z = jnp.where(row < 6, swap4(z) + sign * y, DT * z)
            ref[0, k] = jnp.where(row < 4, ref[0, k], out_y)
            ref[1, k] = jnp.where(row < 4, ref[1, k], out_z)


def odd_ends(s, sf, tf, lo_ref, hi_ref, row, coef, damping, cells):
    m_t, m_f, m_s = masks(1, row, coef, damping)
    keep = 1.0 + m_s
    end_traces_one(s, lo_ref, hi_ref, m_t, row)
    get = lambda comp, a, k: s[comp, 25 * a + k] * m_t
    for k in range(25):
        y = [get(1, a, k) for a in range(5)]
        z = [get(2, a, k) for a in range(5)]
        dy, dz = derive_at_ends(y), derive_at_ends(z)
        for a in ENDS:
            tf[1, a // 4, k] = -dz[a] - swap4(y[a])
            tf[2, a // 4, k] = dy[a] - swap4(z[a])

    def final(a, k, *got):
        for comp in range(3):
            sf[comp, a // 4, k] = s[comp, 25 * a + k] * keep + swap4(got[comp]) * m_f

    yz_into(ENDS, get, tf, lambda a, k: (a // 4, k), cells, final)
    end_traces_two(sf, lo_ref, hi_ref, row)


def inner_kernel(s, aux, si, ci):
    row, lane = iotas()
    cells = Cells(row, lane)
    coef, damping = aux[0], aux[1]
    m_t, m_f, m_s = masks(1, row, coef, damping)
    keep = 1.0 + m_s
    get = lambda comp, a, k: s[comp, 25 * a + k] * m_t
    for k in range(25):
        dy = derive_inside([get(1, a, k) for a in range(5)])
        dz = derive_inside([get(2, a, k) for a in range(5)])
        for a in INSIDE:
            ci[1, 25 * a + k] = -dz[a]
            ci[2, 25 * a + k] = dy[a]

    def final(a, k, *got):
        for comp in range(3):
            si[comp, a - 1, k] = s[comp, 25 * a + k] * keep + swap4(got[comp]) * m_f

    whole = lambda a, k: (25 * a + k,)
    yz_into(INSIDE, get, ci, whole, cells, final)
    m_t2, _, _ = masks(2, row, coef, damping)
    get2 = lambda comp, a, k: si[comp, a - 1, k] * m_t2
    for k in range(25):
        dy = derive_from_inside([None] + [get2(1, a, k) for a in INSIDE])
        dz = derive_from_inside([None] + [get2(2, a, k) for a in INSIDE])
        for a in range(5):
            ci[1, 25 * a + k] = -dz[a]
            ci[2, 25 * a + k] = dy[a]

    def store(a, k, *got):
        for comp in range(3):
            ci[comp, 25 * a + k] = got[comp]

    yz_into(INSIDE, get2, ci, whole, cells, store)


def even_half(sf, si, ci, tf, below, above, lo_own, hi_own, row, m_t, cells, final):
    position, last = lax.axis_index("space"), lax.axis_size("space") - 1
    has = {0: (position > 0).astype(F32), 4: (position < last).astype(F32)}
    to_same = rows(row, 0.0, LIFT, 0.0, 0.0)
    to_primal = rows(row, 0.0, 0.0, LIFT * DT, 0.0)
    to_dual = rows(row, 0.0, 0.0, 0.0, LIFT)
    late_primal = rows(row, 0.0, 0.0, 1.0, 0.0)
    late_dual = rows(row, 0.0, 0.0, 0.0, 1.0)
    fix = rows(row, -LIFT * DT, LIFT * DT, 0.0, 0.0)
    for k in range(25):
        ends = {}
        for a, sign, got, own in ((0, -1.0, below, lo_own), (4, 1.0, above, hi_own)):
            y, z = got(0, k) * has[a], got(1, k) * has[a]
            ry, rz = swap4(y), swap4(z)
            s_y = sf[1, a // 4, k] + (ry * to_primal - sign * (rz * to_dual) + y * to_same)
            s_z = sf[2, a // 4, k] + (rz * to_primal + sign * (ry * to_dual) + z * to_same)
            sf[1, a // 4, k] = s_y
            sf[2, a // 4, k] = s_z
            more = has[a] * fix
            y = y + sign * swap4(own[1, k] * more)
            z = z - sign * swap4(own[0, k] * more)
            ext_y = y * late_primal - sign * (z * late_dual) + swap4(y * late_dual)
            ext_z = z * late_primal + sign * (y * late_dual) + swap4(z * late_dual)
            t_y, t_z = s_y * m_t, s_z * m_t
            ends[a] = (t_y, t_z, ext_y - swap4(t_y), ext_z - swap4(t_z))
        dy = derive_from_ends(ends[0][0], ends[4][0])
        dz = derive_from_ends(ends[0][1], ends[4][1])
        for a in range(5):
            n = 25 * a + k
            got_y, got_z = ci[1, n] - dz[a], ci[2, n] + dy[a]
            if a in ENDS:
                tf[1, a // 4, k] = got_y + ends[a][2]
                tf[2, a // 4, k] = got_z + ends[a][3]
            else:
                final(a, k, ci[0, n], got_y, got_z)
    get = lambda comp, a, k: sf[comp, a // 4, k] * m_t
    yz_into(ENDS, get, tf, lambda a, k: (a // 4, k), cells, final)


def whole_traces(ref):
    return lambda comp, k: ref[comp, k]


def pack_traces(msg, seen, ref, row, side):
    for k in range(25):
        ref[k] = jnp.where(row < 4, msg[0, k], swap4(msg[1, k]))
    for i in range(13):
        k, later = 2 * i, min(2 * i + 1, 24)
        ref[25 + i] = rows(
            row,
            pltpu.roll(msg[0, k], 2, 0),
            swap4(msg[1, k]),
            pltpu.roll(msg[0, later], 6, 0),
            msg[1, later],
        )
    total = Total(jnp.zeros((8, 128), F32))
    for k in range(25):
        for comp in range(2):
            w = LIFT * node_weight(side, k)
            total.add(pltpu.roll(seen[comp, k], 2, 0) * (msg[comp, k] * w))
    ref[38] = swap4(total.value())


def packed_traces(ref, row):
    def plane(comp, k):
        early = ref[k] if comp == 0 else swap4(ref[k])
        shift = ((6, 2), (4, 0))[comp][k % 2]
        late = ref[25 + k // 2]
        late = pltpu.roll(late, shift, 0) if shift else late
        return jnp.where(row < 4, early, jnp.where(row < 6, 0.0, late))

    return plane


def old_plane(sf, si, comp, a, k):
    return sf[comp, a // 4, k] if a in ENDS else si[comp, a - 1, k]


def tree_sum(parts):
    while len(parts) > 1:
        parts = [sum(parts[i : i + 2]) for i in range(0, len(parts), 2)]
    return parts[0]


class Total:
    def __init__(self, zero):
        self.parts, self.turn = [zero] * 8, 0

    def add(self, x):
        self.parts[self.turn] = self.parts[self.turn] + x
        self.turn = (self.turn + 1) % 8

    def value(self):
        return tree_sum(self.parts)


def first_kernel(
    fields, cot, perm_in, reg_in, cond_in, s, sf, lo_ref, hi_ref, aux, tf, perm, reg, cond, sems
):
    row, lane = iotas()
    cells = Cells(row, lane)
    small = [
        pltpu.make_async_copy(src, dst, sems.at[4 + i])
        for i, (src, dst) in enumerate(((perm_in, perm), (reg_in, reg), (cond_in, cond)))
    ]
    copies = [
        pltpu.make_async_copy(src, s.at[:, :, pl.ds(2 * i, 2), :], sems.at[i])
        for i, src in enumerate(
            (fields.at[0:3], cot.at[0:3], fields.at[3:6], cot.at[3:6])
        )
    ]
    for copy in small + copies:
        copy.start()
    for copy in small:
        copy.wait()
    coef, damping = materials(perm, reg, cond, aux)
    for copy in copies:
        copy.wait()
    dual = (row & 2) != 0

    for a in range(5):
        for k in range(25):
            scaled = jnp.where(dual, 1.0 / node_weight(a, k), 1.0)
            for comp in range(3):
                s[comp, 25 * a + k] = s[comp, 25 * a + k] * scaled
    odd_ends(s, sf, tf, lo_ref, hi_ref, row, coef, damping, cells)


def second_kernel(
    sf_in, si, ci, lo_own, hi_own, below, above, aux, layer, cell, node_ref, amp,
    s, sf, lo_ref, hi_ref, g_ref, lo_pack, hi_pack, tf,
):
    row, lane = iotas()
    cells = Cells(row, lane)
    coef, damping = aux[0], aux[1]
    m_t, m_f, m_s = masks(2, row, coef, damping)
    total = Total(jnp.zeros((8, 128), F32))

    def final(a, k, *got):
        for comp in range(3):
            old = old_plane(sf, si, comp, a, k)
            inc = swap4(got[comp]) * m_f + old * m_s
            new = old + inc
            s[comp, 25 * a + k] = new
            total.add(pltpu.roll(inc, 2, 0) * (new * node_weight(a, k)))

    even_half(sf, si, ci, tf, whole_traces(below), whole_traces(above), lo_own, hi_own, row, m_t, cells, final)
    g = total.value()
    node = node_ref[0]
    w = weight_at(node // 25) * weight_at((node // 5) % 5) * weight_at(node % 5)
    incs = source_planes(0, layer, cell, amp, row, lane, coef)
    for comp in range(3):
        new = s[comp, node] + incs[comp]
        s[comp, node] = new
        g = g + pltpu.roll(incs[comp], 2, 0) * (new * w)
    g_ref[...] = g
    odd_ends(s, sf, tf, lo_ref, hi_ref, row, coef, damping, cells)
    pack_traces(lo_ref, below, lo_pack, row, 0)
    pack_traces(hi_ref, above, hi_pack, row, 4)


def third_kernel(
    sf_in, si, ci, lo_own, hi_own, below, above, aux, g_in, layer, cell, node_ref, amp, cot,
    s, g_ref, sf, tf,
):
    row, lane = iotas()
    cells = Cells(row, lane)
    coef, damping = aux[0], aux[1]
    m_t, m_f, m_s = masks(2, row, coef, damping)
    total = Total(jnp.zeros((2, 128), F32))

    def final(a, k, *got):
        for comp in range(3):
            old = old_plane(sf, si, comp, a, k)
            inc = swap4(got[comp]) * m_f + old * m_s
            s[comp, 25 * a + k] = (old + inc) * node_weight(a, k)
            total.add(inc[0:2] * cot[comp, 25 * a + k])

    even_half(
        sf, si, ci, tf, packed_traces(below, row), packed_traces(above, row), lo_own, hi_own, row, m_t, cells, final
    )
    g = total.value()
    node = node_ref[0]
    incs = source_planes(1, layer, cell, amp, row, lane, coef)
    for comp in range(3):
        g = g + incs[comp][0:2] * cot[comp, node]
    position, last = lax.axis_index("space"), lax.axis_size("space") - 1
    g = g + below[38, 0:2] * (position > 0).astype(F32)
    g = g + above[38, 0:2] * (position < last).astype(F32)
    g = g + g_in[2:4]
    g_ref[...] = g * coef[0:2] * (-1.0 / DT)


def store_kernel(s, adj, sems):
    stores = [
        pltpu.make_async_copy(
            s.at[:, :, pl.ds(2 + 4 * i, 2), :], adj.at[3 * i : 3 * i + 3], sems.at[i]
        )
        for i in range(2)
    ]
    for store in stores:
        store.start()
    for store in stores:
        store.wait()


def struct(*shape):
    return jax.ShapeDtypeStruct(shape, F32)


VMEM = pl.BlockSpec(memory_space=pltpu.VMEM)
SMEM = pl.BlockSpec(memory_space=pltpu.SMEM)
HBM = pl.BlockSpec(memory_space=pltpu.HBM)
PARAMS = pltpu.CompilerParams(vmem_limit_bytes=24 * 1024 * 1024)
STATE = (3, 125, 8, 128)
FACES = (3, 2, 25, 8, 128)
INNER = (3, 3, 25, 8, 128)
TRACE = (2, 25, 8, 128)
PACKED = (39, 8, 128)


def exchange(lo, hi):
    peers = lax.axis_size("space")
    even = lax.axis_index("space") % 2 == 0
    inner_pairs = [(i, i ^ 1) for i in range(peers)]
    outer_pairs = [(i, (i + 2 * (i % 2) - 1) % peers) for i in range(peers)]
    one, two = lax.optimization_barrier((jnp.where(even, lo, hi), jnp.where(even, hi, lo)))
    got_one = lax.ppermute(one, "space", outer_pairs)
    got_two = lax.ppermute(two, "space", inner_pairs)
    return jnp.where(even, got_one, got_two), jnp.where(even, got_two, got_one)


def src_sum(x):
    for group in ((1, 2, 3), (4, 8, 12)):
        got = [lax.ppermute(x, "src", [(i, i ^ d) for i in range(16)]) for d in group]
        x = (x + got[0]) + (got[1] + got[2])
    return x


def on_device(
    fields, cotangent, permittivity, regions, conductance, src_layer, src_cell, src_node, src_amp
):
    wide = fields.shape[:2] + (2, 128)
    f = fields.reshape(wide)
    cot = cotangent.reshape(wide)
    perm = permittivity.reshape(2, 128)
    reg = regions.reshape(2, 128)
    f, cot, perm, reg, conductance = (
        pltpu.with_memory_space_constraint(x, pltpu.HBM) for x in (f, cot, perm, reg, conductance)
    )
    source = (src_layer, src_cell, src_node, src_amp)
    inner = pl.pallas_call(
        inner_kernel,
        out_shape=(struct(*INNER), struct(*STATE)),
        in_specs=[VMEM] * 2,
        out_specs=[VMEM] * 2,
        compiler_params=PARAMS,
        cost_estimate=pl.CostEstimate(flops=20_000_000, bytes_accessed=1000, transcendentals=0),
        name="inner",
    )
    s, sf, lo, hi, aux = pl.pallas_call(
        first_kernel,
        out_shape=(struct(*STATE), struct(*FACES), struct(*TRACE), struct(*TRACE), struct(2, 8, 128)),
        in_specs=[HBM] * 5,
        out_specs=[VMEM] * 5,
        scratch_shapes=[
            pltpu.VMEM(FACES, F32),
            pltpu.VMEM((2, 128), F32),
            pltpu.VMEM((2, 128), jnp.int32),
            pltpu.SMEM((8,), F32),
            pltpu.SemaphoreType.DMA((7,)),
        ],
        compiler_params=PARAMS,
        name="first",
    )(f, cot, perm, reg, conductance)
    below, above = exchange(lo, hi)
    si, ci = inner(s, aux)
    s, sf, lo, hi, g, lo_pack, hi_pack = pl.pallas_call(
        second_kernel,
        out_shape=(
            struct(*STATE),
            struct(*FACES),
            struct(*TRACE),
            struct(*TRACE),
            struct(8, 128),
            struct(*PACKED),
            struct(*PACKED),
        ),
        in_specs=[VMEM] * 8 + [SMEM] * 4,
        out_specs=[VMEM] * 7,
        input_output_aliases={0: 1},
        scratch_shapes=[pltpu.VMEM(FACES, F32)],
        compiler_params=PARAMS,
        name="second",
    )(sf, si, ci, lo, hi, below, above, aux, *source)
    below, above = exchange(lo_pack, hi_pack)
    si, ci = inner(s, aux)
    s, g, _ = pl.pallas_call(
        third_kernel,
        out_shape=(struct(*STATE), struct(2, 128), struct(*FACES)),
        in_specs=[VMEM] * 9 + [SMEM] * 4 + [VMEM],
        out_specs=[VMEM] * 3,
        input_output_aliases={0: 2},
        scratch_shapes=[pltpu.VMEM(FACES, F32)],
        compiler_params=PARAMS,
        name="third",
    )(sf, si, ci, lo, hi, below, above, aux, g, *source, cotangent.reshape(wide))
    adjoint = pl.pallas_call(
        store_kernel,
        out_shape=struct(*wide),
        in_specs=[VMEM],
        out_specs=HBM,
        scratch_shapes=[pltpu.SemaphoreType.DMA((2,))],
        compiler_params=PARAMS,
        cost_estimate=pl.CostEstimate(flops=0, bytes_accessed=4_000_000, transcendentals=0),
        name="store",
    )(s)
    gradient = src_sum(g).reshape(permittivity.shape)
    adjoint = with_layout_constraint(adjoint.reshape(fields.shape), Layout((0, 1, 2, 3, 4)))
    return adjoint, gradient


def solution(mesh):
    return jax.shard_map(
        on_device,
        mesh=mesh,
        in_specs=(
            P(None, None, "src", "space", None),
            P(None, None, "src", "space", None),
            P("space", None),
            P("space", None),
            P(),
            P("src"),
            P("src"),
            P("src"),
            P("src", None),
        ),
        out_specs=(P(None, None, "src", "space", None), P("space", None)),
        check_vma=False,
    )
```

```python
import math

import jax
import jax.numpy as jnp
import numpy as np
from jax import lax
from jax.experimental import pallas as pl
from jax.experimental.layout import Layout, with_layout_constraint
from jax.experimental.pallas import tpu as pltpu
from jax.sharding import PartitionSpec as P

EZ = 16
DT = 0.02
LIFT = 10.0
METRIC = 2.0
F32 = jnp.float32


WEIGHTS = (1.0 / 10.0, 49.0 / 90.0, 32.0 / 45.0, 49.0 / 90.0, 1.0 / 10.0)


def central_matrix():
    points = np.array([-1.0, -math.sqrt(3.0 / 7.0), 0.0, math.sqrt(3.0 / 7.0), 1.0])
    products = [
        np.prod([points[i] - points[j] for j in range(5) if j != i]) for i in range(5)
    ]
    matrix = np.zeros((5, 5))
    for i in range(5):
        for j in range(5):
            if j != i:
                matrix[i, j] = products[i] / (products[j] * (points[i] - points[j]))
    for i in range(5):
        matrix[i, i] = -np.sum(matrix[i])
    return (METRIC * matrix + np.diag([LIFT, 0.0, 0.0, 0.0, -LIFT])) / LIFT


CENTRAL = central_matrix()


def halves():
    d = CENTRAL
    h = [[float(0.5 * (d[i, j] - d[i, 4 - j])) for j in range(2)] for i in range(2)]
    g = [[float(0.5 * (d[i, j] + d[i, 4 - j])) for j in range(2)] for i in range(2)]
    return h, g, [float(d[i, 2]) for i in range(2)], [float(d[2, j]) for j in range(2)]


ODD, EVEN, MIDDLE, CENTRE = halves()


def derive(u):
    e0, e1, m = u[0] + u[4], u[1] + u[3], u[2]
    o0, o1 = u[0] - u[4], u[1] - u[3]
    s0 = ODD[0][0] * o0 + ODD[0][1] * o1
    s1 = ODD[1][0] * o0 + ODD[1][1] * o1
    d0 = EVEN[0][0] * e0 + EVEN[0][1] * e1 + MIDDLE[0] * m
    d1 = EVEN[1][0] * e0 + EVEN[1][1] * e1 + MIDDLE[1] * m
    mid = CENTRE[0] * o0 + CENTRE[1] * o1
    return [s0 + d0, s1 + d1, mid, s1 - d1, s0 - d0]


def derive_at_ends(u):
    e0, e1, m = u[0] + u[4], u[1] + u[3], u[2]
    o0, o1 = u[0] - u[4], u[1] - u[3]
    s0 = ODD[0][0] * o0 + ODD[0][1] * o1
    d0 = EVEN[0][0] * e0 + EVEN[0][1] * e1 + MIDDLE[0] * m
    return {0: s0 + d0, 4: s0 - d0}


def derive_inside(u):
    e0, e1, m = u[0] + u[4], u[1] + u[3], u[2]
    o0, o1 = u[0] - u[4], u[1] - u[3]
    s1 = ODD[1][0] * o0 + ODD[1][1] * o1
    d1 = EVEN[1][0] * e0 + EVEN[1][1] * e1 + MIDDLE[1] * m
    mid = CENTRE[0] * o0 + CENTRE[1] * o1
    return {1: s1 + d1, 2: mid, 3: s1 - d1}


def derive_from_inside(u):
    e1, o1, m = u[1] + u[3], u[1] - u[3], u[2]
    s0, s1 = ODD[0][1] * o1, ODD[1][1] * o1
    d0 = EVEN[0][1] * e1 + MIDDLE[0] * m
    d1 = EVEN[1][1] * e1 + MIDDLE[1] * m
    return [s0 + d0, s1 + d1, CENTRE[1] * o1, s1 - d1, s0 - d0]


def derive_from_ends(u0, u4):
    e0, o0 = u0 + u4, u0 - u4
    s0, s1 = ODD[0][0] * o0, ODD[1][0] * o0
    d0, d1 = EVEN[0][0] * e0, EVEN[1][0] * e0
    return [s0 + d0, s1 + d1, CENTRE[0] * o0, s1 - d1, s0 - d0]


def swap4(x):
    return pltpu.roll(x, 4, 0)


def iotas():
    row = lax.broadcasted_iota(jnp.int32, (8, 128), 0)
    lane = lax.broadcasted_iota(jnp.int32, (8, 128), 1)
    return row, lane


def rows(row, v0, v1, v2, v3):
    return jnp.where(row < 2, v0, jnp.where(row < 4, v1, jnp.where(row < 6, v2, v3)))


class Cells:
    def __init__(self, row, lane):
        self.even = (row & 1) == 0
        self.y_last = lane >= 112
        self.y_first = lane < 16
        self.z_last = (lane & 15) == 15
        self.z_first = (lane & 15) == 0

    def other_half(self, x):
        return jnp.where(self.even, pltpu.roll(x, 7, 0), pltpu.roll(x, 1, 0))

    def y_up(self, x):
        x = pltpu.roll(x, 112, 1)
        return jnp.where(self.y_last, self.other_half(x), x)

    def y_down(self, x):
        x = pltpu.roll(x, 16, 1)
        return jnp.where(self.y_first, self.other_half(x), x)

    def z_up(self, x):
        return jnp.where(self.z_last, pltpu.roll(x, 15, 1), pltpu.roll(x, 127, 1))

    def z_down(self, x):
        return jnp.where(self.z_first, pltpu.roll(x, 113, 1), pltpu.roll(x, 1, 1))


ENDS, INSIDE = (0, 4), (1, 2, 3)


def node_weight(a, k):
    return WEIGHTS[a] * WEIGHTS[k // 5] * WEIGHTS[k % 5]


def weight_at(i):
    return jnp.where((i == 0) | (i == 4), WEIGHTS[0], jnp.where(i == 2, WEIGHTS[2], WEIGHTS[1]))


def penalty(inner, outer):
    return swap4(outer - inner)


def y_lines(planes, get, add, cells):
    for a in planes:
        for c in range(5):
            z = [get(2, a, 5 * b + c) for b in range(5)]
            x = [get(0, a, 5 * b + c) for b in range(5)]
            out_x, out_z = derive(z), [-v for v in derive(x)]
            oz, ox = cells.y_down(z[4]), cells.y_down(x[4])
            out_x[0] = out_x[0] - oz + penalty(x[0], ox)
            out_z[0] = out_z[0] + ox + penalty(z[0], oz)
            oz, ox = cells.y_up(z[0]), cells.y_up(x[0])
            out_x[4] = out_x[4] + oz + penalty(x[4], ox)
            out_z[4] = out_z[4] - ox + penalty(z[4], oz)
            for b in range(5):
                add(a, 5 * b + c, out_x[b], out_z[b])


def z_lines(planes, get, add, cells):
    for a in planes:
        for b in range(5):
            x = [get(0, a, 5 * b + c) for c in range(5)]
            y = [get(1, a, 5 * b + c) for c in range(5)]
            out_y, out_x = derive(x), [-v for v in derive(y)]
            ox, oy = cells.z_down(x[4]), cells.z_down(y[4])
            out_y[0] = out_y[0] - ox + penalty(y[0], oy)
            out_x[0] = out_x[0] + oy + penalty(x[0], ox)
            ox, oy = cells.z_up(x[0]), cells.z_up(y[0])
            out_y[4] = out_y[4] + ox + penalty(y[4], oy)
            out_x[4] = out_x[4] - oy + penalty(x[4], ox)
            for c in range(5):
                add(a, 5 * b + c, out_x[c], out_y[c])


def yz_into(planes, get, t, where, cells, final):
    def add_y(a, k, x, z):
        i = where(a, k)
        t[(0, *i)] = x
        t[(2, *i)] = t[(2, *i)] + z

    def add_z(a, k, x, y):
        i = where(a, k)
        final(a, k, t[(0, *i)] + x, t[(1, *i)] + y, t[(2, *i)])

    for a in planes:
        y_lines((a,), get, add_y, cells)
        z_lines((a,), get, add_z, cells)


def masks(parity, row, coef, damping):
    if parity == 1:
        m_t = rows(row, 1.0, coef, -1.0, 0.0)
        m_f = rows(row, 0.0, LIFT, -LIFT * DT, LIFT)
        m_s = rows(row, 0.0, -damping * coef, 0.0, 0.0)
    else:
        m_t = rows(row, 1.0, 0.0, 1.0, DT)
        m_f = rows(row, LIFT * coef, -LIFT, 0.0, LIFT)
        m_s = rows(row, -damping * coef, 0.0, 0.0, 0.0)
    return m_t, m_f, m_s


def materials(perm, reg, cond, aux):
    two = lambda x: jnp.concatenate([x, x, x, x], axis=0)
    perm, reg = perm[...], reg[...]
    damping = jnp.zeros((2, 128), F32)
    for r in range(8):
        damping = jnp.where(reg == r, cond[r], damping)
    coef, damping = two(DT / perm), two(damping)
    aux[0], aux[1] = coef, damping
    return coef, damping


def source_planes(step, layer, cell, amp, row, lane, coef):
    here = layer[0] == lax.axis_index("space")
    place = (row < 2) & ((row & 1) * 128 + lane == cell[0])
    shape = jnp.where(place, coef, 0.0)
    return [shape * jnp.where(here, amp[0, 3 * step + i], 0.0) for i in range(3)]


def end_traces_one(s, lo_ref, hi_ref, m_t, row):
    for k in range(25):
        for a, sign, ref in ((0, 1.0, lo_ref), (4, -1.0, hi_ref)):
            y, z = s[1, 25 * a + k] * m_t, s[2, 25 * a + k] * m_t
            ref[0, k] = jnp.where(row < 2, sign * z - swap4(y), y)
            ref[1, k] = jnp.where(row < 2, -sign * y - swap4(z), z)


def end_traces_two(sf, lo_ref, hi_ref, row):
    for k in range(25):
        for side, sign, ref in ((0, 1.0, lo_ref), (1, -1.0, hi_ref)):
            y, z = sf[1, side, k], sf[2, side, k]
            out_y = jnp.where(row < 6, swap4(y) - sign * z, DT * y)
            out_z = jnp.where(row < 6, swap4(z) + sign * y, DT * z)
            ref[0, k] = jnp.where(row < 4, ref[0, k], out_y)
            ref[1, k] = jnp.where(row < 4, ref[1, k], out_z)


def odd_ends(s, sf, tf, lo_ref, hi_ref, row, coef, damping, cells):
    m_t, m_f, m_s = masks(1, row, coef, damping)
    keep = 1.0 + m_s
    end_traces_one(s, lo_ref, hi_ref, m_t, row)
    get = lambda comp, a, k: s[comp, 25 * a + k] * m_t
    for k in range(25):
        y = [get(1, a, k) for a in range(5)]
        z = [get(2, a, k) for a in range(5)]
        dy, dz = derive_at_ends(y), derive_at_ends(z)
        for a in ENDS:
            tf[1, a // 4, k] = -dz[a] - swap4(y[a])
            tf[2, a // 4, k] = dy[a] - swap4(z[a])

    def final(a, k, *got):
        for comp in range(3):
            sf[comp, a // 4, k] = s[comp, 25 * a + k] * keep + swap4(got[comp]) * m_f

    yz_into(ENDS, get, tf, lambda a, k: (a // 4, k), cells, final)
    end_traces_two(sf, lo_ref, hi_ref, row)


def inner_kernel(s, aux, si, ci):
    row, lane = iotas()
    cells = Cells(row, lane)
    coef, damping = aux[0], aux[1]
    m_t, m_f, m_s = masks(1, row, coef, damping)
    keep = 1.0 + m_s
    get = lambda comp, a, k: s[comp, 25 * a + k] * m_t
    for k in range(25):
        dy = derive_inside([get(1, a, k) for a in range(5)])
        dz = derive_inside([get(2, a, k) for a in range(5)])
        for a in INSIDE:
            ci[1, 25 * a + k] = -dz[a]
            ci[2, 25 * a + k] = dy[a]

    def final(a, k, *got):
        for comp in range(3):
            si[comp, a - 1, k] = s[comp, 25 * a + k] * keep + swap4(got[comp]) * m_f

    whole = lambda a, k: (25 * a + k,)
    yz_into(INSIDE, get, ci, whole, cells, final)
    m_t2, _, _ = masks(2, row, coef, damping)
    get2 = lambda comp, a, k: si[comp, a - 1, k] * m_t2
    for k in range(25):
        dy = derive_from_inside([None] + [get2(1, a, k) for a in INSIDE])
        dz = derive_from_inside([None] + [get2(2, a, k) for a in INSIDE])
        for a in range(5):
            ci[1, 25 * a + k] = -dz[a]
            ci[2, 25 * a + k] = dy[a]

    def store(a, k, *got):
        for comp in range(3):
            ci[comp, 25 * a + k] = got[comp]

    yz_into(INSIDE, get2, ci, whole, cells, store)


def even_half(sf, si, ci, tf, below, above, lo_own, hi_own, row, m_t, cells, final):
    position, last = lax.axis_index("space"), lax.axis_size("space") - 1
    has = {0: (position > 0).astype(F32), 4: (position < last).astype(F32)}
    to_same = rows(row, 0.0, LIFT, 0.0, 0.0)
    to_primal = rows(row, 0.0, 0.0, LIFT * DT, 0.0)
    to_dual = rows(row, 0.0, 0.0, 0.0, LIFT)
    late_primal = rows(row, 0.0, 0.0, 1.0, 0.0)
    late_dual = rows(row, 0.0, 0.0, 0.0, 1.0)
    fix = rows(row, -LIFT * DT, LIFT * DT, 0.0, 0.0)
    for k in range(25):
        ends = {}
        for a, sign, got, own in ((0, -1.0, below, lo_own), (4, 1.0, above, hi_own)):
            y, z = got(0, k) * has[a], got(1, k) * has[a]
            ry, rz = swap4(y), swap4(z)
            s_y = sf[1, a // 4, k] + (ry * to_primal - sign * (rz * to_dual) + y * to_same)
            s_z = sf[2, a // 4, k] + (rz * to_primal + sign * (ry * to_dual) + z * to_same)
            sf[1, a // 4, k] = s_y
            sf[2, a // 4, k] = s_z
            more = has[a] * fix
            y = y + sign * swap4(own[1, k] * more)
            z = z - sign * swap4(own[0, k] * more)
            ext_y = y * late_primal - sign * (z * late_dual) + swap4(y * late_dual)
            ext_z = z * late_primal + sign * (y * late_dual) + swap4(z * late_dual)
            t_y, t_z = s_y * m_t, s_z * m_t
            ends[a] = (t_y, t_z, ext_y - swap4(t_y), ext_z - swap4(t_z))
        dy = derive_from_ends(ends[0][0], ends[4][0])
        dz = derive_from_ends(ends[0][1], ends[4][1])
        for a in range(5):
            n = 25 * a + k
            got_y, got_z = ci[1, n] - dz[a], ci[2, n] + dy[a]
            if a in ENDS:
                tf[1, a // 4, k] = got_y + ends[a][2]
                tf[2, a // 4, k] = got_z + ends[a][3]
            else:
                final(a, k, ci[0, n], got_y, got_z)
    get = lambda comp, a, k: sf[comp, a // 4, k] * m_t
    yz_into(ENDS, get, tf, lambda a, k: (a // 4, k), cells, final)


def whole_traces(ref):
    return lambda comp, k: ref[comp, k]


def pack_traces(msg, seen, ref, row, side):
    for k in range(25):
        ref[k] = jnp.where(row < 4, msg[0, k], swap4(msg[1, k]))
    for i in range(13):
        k, later = 2 * i, min(2 * i + 1, 24)
        ref[25 + i] = rows(
            row,
            pltpu.roll(msg[0, k], 2, 0),
            swap4(msg[1, k]),
            pltpu.roll(msg[0, later], 6, 0),
            msg[1, later],
        )
    total = Total(jnp.zeros((8, 128), F32))
    for k in range(25):
        for comp in range(2):
            w = LIFT * node_weight(side, k)
            total.add(pltpu.roll(seen[comp, k], 2, 0) * (msg[comp, k] * w))
    ref[38] = swap4(total.value())


def packed_traces(ref, row):
    def plane(comp, k):
        early = ref[k] if comp == 0 else swap4(ref[k])
        shift = ((6, 2), (4, 0))[comp][k % 2]
        late = ref[25 + k // 2]
        late = pltpu.roll(late, shift, 0) if shift else late
        return jnp.where(row < 4, early, jnp.where(row < 6, 0.0, late))

    return plane


def old_plane(sf, si, comp, a, k):
    return sf[comp, a // 4, k] if a in ENDS else si[comp, a - 1, k]


def tree_sum(parts):
    while len(parts) > 1:
        parts = [sum(parts[i : i + 2]) for i in range(0, len(parts), 2)]
    return parts[0]


class Total:
    def __init__(self, zero):
        self.parts, self.turn = [zero] * 8, 0

    def add(self, x):
        self.parts[self.turn] = self.parts[self.turn] + x
        self.turn = (self.turn + 1) % 8

    def value(self):
        return tree_sum(self.parts)


def first_kernel(
    fields, cot, perm_in, reg_in, cond_in, s, sf, lo_ref, hi_ref, aux, tf, perm, reg, cond, sems
):
    row, lane = iotas()
    cells = Cells(row, lane)
    small = [
        pltpu.make_async_copy(src, dst, sems.at[4 + i])
        for i, (src, dst) in enumerate(((perm_in, perm), (reg_in, reg), (cond_in, cond)))
    ]
    copies = [
        pltpu.make_async_copy(src, s.at[:, :, pl.ds(2 * i, 2), :], sems.at[i])
        for i, src in enumerate(
            (fields.at[0:3], cot.at[0:3], fields.at[3:6], cot.at[3:6])
        )
    ]
    for copy in small + copies:
        copy.start()
    for copy in small:
        copy.wait()
    coef, damping = materials(perm, reg, cond, aux)
    for copy in copies:
        copy.wait()
    dual = (row & 2) != 0

    for a in range(5):
        for k in range(25):
            scaled = jnp.where(dual, 1.0 / node_weight(a, k), 1.0)
            for comp in range(3):
                s[comp, 25 * a + k] = s[comp, 25 * a + k] * scaled
    odd_ends(s, sf, tf, lo_ref, hi_ref, row, coef, damping, cells)


def second_kernel(
    sf_in, si, ci, lo_own, hi_own, below, above, aux, layer, cell, node_ref, amp,
    s, sf, lo_ref, hi_ref, g_ref, lo_pack, hi_pack, tf,
):
    row, lane = iotas()
    cells = Cells(row, lane)
    coef, damping = aux[0], aux[1]
    m_t, m_f, m_s = masks(2, row, coef, damping)
    total = Total(jnp.zeros((8, 128), F32))

    def final(a, k, *got):
        for comp in range(3):
            old = old_plane(sf, si, comp, a, k)
            inc = swap4(got[comp]) * m_f + old * m_s
            new = old + inc
            s[comp, 25 * a + k] = new
            total.add(pltpu.roll(inc, 2, 0) * (new * node_weight(a, k)))

    even_half(sf, si, ci, tf, whole_traces(below), whole_traces(above), lo_own, hi_own, row, m_t, cells, final)
    g = total.value()
    node = node_ref[0]
    w = weight_at(node // 25) * weight_at((node // 5) % 5) * weight_at(node % 5)
    incs = source_planes(0, layer, cell, amp, row, lane, coef)
    for comp in range(3):
        new = s[comp, node] + incs[comp]
        s[comp, node] = new
        g = g + pltpu.roll(incs[comp], 2, 0) * (new * w)
    g_ref[...] = g
    odd_ends(s, sf, tf, lo_ref, hi_ref, row, coef, damping, cells)
    pack_traces(lo_ref, below, lo_pack, row, 0)
    pack_traces(hi_ref, above, hi_pack, row, 4)


def third_kernel(
    sf_in, si, ci, lo_own, hi_own, below, above, aux, g_in, layer, cell, node_ref, amp, cot,
    s, g_ref, sf, tf,
):
    row, lane = iotas()
    cells = Cells(row, lane)
    coef, damping = aux[0], aux[1]
    m_t, m_f, m_s = masks(2, row, coef, damping)
    total = Total(jnp.zeros((2, 128), F32))

    def final(a, k, *got):
        for comp in range(3):
            old = old_plane(sf, si, comp, a, k)
            inc = swap4(got[comp]) * m_f + old * m_s
            s[comp, 25 * a + k] = (old + inc) * node_weight(a, k)
            total.add(inc[0:2] * cot[comp, 25 * a + k])

    even_half(
        sf, si, ci, tf, packed_traces(below, row), packed_traces(above, row), lo_own, hi_own, row, m_t, cells, final
    )
    g = total.value()
    node = node_ref[0]
    incs = source_planes(1, layer, cell, amp, row, lane, coef)
    for comp in range(3):
        g = g + incs[comp][0:2] * cot[comp, node]
    position, last = lax.axis_index("space"), lax.axis_size("space") - 1
    g = g + below[38, 0:2] * (position > 0).astype(F32)
    g = g + above[38, 0:2] * (position < last).astype(F32)
    g = g + g_in[2:4]
    g_ref[...] = g * coef[0:2] * (-1.0 / DT)


def store_kernel(s, adj, sems):
    stores = [
        pltpu.make_async_copy(
            s.at[:, :, pl.ds(2 + 4 * i, 2), :], adj.at[3 * i : 3 * i + 3], sems.at[i]
        )
        for i in range(2)
    ]
    for store in stores:
        store.start()
    for store in stores:
        store.wait()


def struct(*shape):
    return jax.ShapeDtypeStruct(shape, F32)


VMEM = pl.BlockSpec(memory_space=pltpu.VMEM)
SMEM = pl.BlockSpec(memory_space=pltpu.SMEM)
HBM = pl.BlockSpec(memory_space=pltpu.HBM)
PARAMS = pltpu.CompilerParams(vmem_limit_bytes=24 * 1024 * 1024)
STATE = (3, 125, 8, 128)
FACES = (3, 2, 25, 8, 128)
INNER = (3, 3, 25, 8, 128)
TRACE = (2, 25, 8, 128)
PACKED = (39, 8, 128)


def exchange(lo, hi):
    peers = lax.axis_size("space")
    even = lax.axis_index("space") % 2 == 0
    inner_pairs = [(i, i ^ 1) for i in range(peers)]
    outer_pairs = [(i, i + 2 * (i % 2) - 1) for i in range(1, peers - 1)]
    one, two = lax.optimization_barrier((jnp.where(even, lo, hi), jnp.where(even, hi, lo)))
    got_one = lax.ppermute(one, "space", outer_pairs)
    got_two = lax.ppermute(two, "space", inner_pairs)
    return jnp.where(even, got_one, got_two), jnp.where(even, got_two, got_one)


def src_sum(x):
    for group in ((1, 2, 3), (4, 8, 12)):
        got = [lax.ppermute(x, "src", [(i, i ^ d) for i in range(16)]) for d in group]
        x = (x + got[0]) + (got[1] + got[2])
    return x


def on_device(
    fields, cotangent, permittivity, regions, conductance, src_layer, src_cell, src_node, src_amp
):
    wide = fields.shape[:2] + (2, 128)
    f = fields.reshape(wide)
    cot = cotangent.reshape(wide)
    perm = permittivity.reshape(2, 128)
    reg = regions.reshape(2, 128)
    f, cot, perm, reg, conductance = (
        pltpu.with_memory_space_constraint(x, pltpu.HBM) for x in (f, cot, perm, reg, conductance)
    )
    source = (src_layer, src_cell, src_node, src_amp)
    inner = pl.pallas_call(
        inner_kernel,
        out_shape=(struct(*INNER), struct(*STATE)),
        in_specs=[VMEM] * 2,
        out_specs=[VMEM] * 2,
        compiler_params=PARAMS,
        cost_estimate=pl.CostEstimate(flops=20_000_000, bytes_accessed=1000, transcendentals=0),
        name="inner",
    )
    s, sf, lo, hi, aux = pl.pallas_call(
        first_kernel,
        out_shape=(struct(*STATE), struct(*FACES), struct(*TRACE), struct(*TRACE), struct(2, 8, 128)),
        in_specs=[HBM] * 5,
        out_specs=[VMEM] * 5,
        scratch_shapes=[
            pltpu.VMEM(FACES, F32),
            pltpu.VMEM((2, 128), F32),
            pltpu.VMEM((2, 128), jnp.int32),
            pltpu.SMEM((8,), F32),
            pltpu.SemaphoreType.DMA((7,)),
        ],
        compiler_params=PARAMS,
        name="first",
    )(f, cot, perm, reg, conductance)
    below, above = exchange(lo, hi)
    si, ci = inner(s, aux)
    s, sf, lo, hi, g, lo_pack, hi_pack = pl.pallas_call(
        second_kernel,
        out_shape=(
            struct(*STATE),
            struct(*FACES),
            struct(*TRACE),
            struct(*TRACE),
            struct(8, 128),
            struct(*PACKED),
            struct(*PACKED),
        ),
        in_specs=[VMEM] * 8 + [SMEM] * 4,
        out_specs=[VMEM] * 7,
        input_output_aliases={0: 1},
        scratch_shapes=[pltpu.VMEM(FACES, F32)],
        compiler_params=PARAMS,
        name="second",
    )(sf, si, ci, lo, hi, below, above, aux, *source)
    below, above = exchange(lo_pack, hi_pack)
    si, ci = inner(s, aux)
    s, g, _ = pl.pallas_call(
        third_kernel,
        out_shape=(struct(*STATE), struct(2, 128), struct(*FACES)),
        in_specs=[VMEM] * 9 + [SMEM] * 4 + [VMEM],
        out_specs=[VMEM] * 3,
        input_output_aliases={0: 2},
        scratch_shapes=[pltpu.VMEM(FACES, F32)],
        compiler_params=PARAMS,
        name="third",
    )(sf, si, ci, lo, hi, below, above, aux, g, *source, cotangent.reshape(wide))
    adjoint = pl.pallas_call(
        store_kernel,
        out_shape=struct(*wide),
        in_specs=[VMEM],
        out_specs=HBM,
        scratch_shapes=[pltpu.SemaphoreType.DMA((2,))],
        compiler_params=PARAMS,
        cost_estimate=pl.CostEstimate(flops=0, bytes_accessed=4_000_000, transcendentals=0),
        name="store",
    )(s)
    gradient = src_sum(g).reshape(permittivity.shape)
    adjoint = with_layout_constraint(adjoint.reshape(fields.shape), Layout((0, 1, 2, 3, 4)))
    return adjoint, gradient


def solution(mesh):
    return jax.shard_map(
        on_device,
        mesh=mesh,
        in_specs=(
            P(None, None, "src", "space", None),
            P(None, None, "src", "space", None),
            P("space", None),
            P("space", None),
            P(),
            P("src"),
            P("src"),
            P("src"),
            P("src", None),
        ),
        out_specs=(P(None, None, "src", "space", None), P("space", None)),
        check_vma=False,
    )
```
